128 devices in a mesh: leaf: 16 (over x_hi, z, core), load: 8 (over x_lo, y).
Axes of the slice: x: 4 (x_hi: 2, x_lo: 2; x = x_hi * 2 + x_lo), y: 4, z: 4, core: 2. Of those that a mesh axis runs over, the one named last changes fastest.
Arguments:
- rhs_leaves: bfloat16 [384, 256, 4096], P('leaf', None, 'load'), may hold values from -6 to 6
- rhs_roots: bfloat16 [16, 256, 4096], P('leaf', None, 'load'), may hold values from -6 to 6
- rhs_seps: bfloat16 [16, 256, 4096], P('leaf', None, 'load'), may hold values from -6 to 6
- above_solution: bfloat16 [256, 4096], P(None, 'load'), may hold values from -6 to 6
- leaf_inverse: bfloat16 [384, 256, 256], P('leaf', 'load'), may hold values from -0.375 to 0.375
- leaf_update: bfloat16 [384, 128, 256], P('leaf', 'load'), may hold values from -0.109375 to 0.109375
- leaf_rows: int32 [384, 128], P('leaf'), may hold values from 0 to 255, as said below
- root_inverse: bfloat16 [16, 256, 256], P('leaf', 'load'), may hold values from -0.375 to 0.375
- root_coupling: bfloat16 [16, 256, 256], P('leaf', 'load'), may hold values from -0.25 to 0.25
- sep_inverse: bfloat16 [16, 256, 256], P('leaf', 'load'), may hold values from -0.375 to 0.375
- sep_coupling: bfloat16 [16, 256, 256], P('leaf', 'load'), may hold values from -0.25 to 0.25
Outputs:
- solution_leaves: bfloat16 [384, 256, 4096], P('leaf', None, 'load')
- solution_roots: bfloat16 [16, 256, 4096], P('leaf', None, 'load')
- solution_seps: bfloat16 [16, 256, 4096], P('leaf', None, 'load')
The draws below stay inside these ranges and needn't reach their ends.
Inputs may be any that keep to these rules, and one draw needn't show every extreme that they name: `leaf_rows`: each row names 128 different rows of its subtree root's 256 unknowns.
All inputs are finite; a program needn't handle non-finite values.
Results may differ from the reference program's by a relative error of at most 0.023.
Values may be sent and summed in bfloat16 or wider, within the bound.
No kernel may reach another device: no remote copies, remote signals or barrier semaphores. Data moves between devices by JAX's collectives and lax.ppermute only.
A program may use at most 128 MiB of HBM per device.

```python
import jax
import jax.numpy as jnp
import numpy as np
from jax import lax

W = 256
K = 128
NS = 24
NRHS = 4096
LEAVES = 384
ROOTS = 16


def draw_leaf_rows(key, part):
    key = jax.random.fold_in(key, 7)
    keys = jax.random.split(key, LEAVES)

    def one_row(row_key, parity):
        order = jax.random.permutation(row_key, W).astype(jnp.int32)
        offset = jnp.where(parity == 0, W - 1 - order[0], W - order[0])
        return ((order + offset) % W)[:K]
    parities = jnp.arange(LEAVES, dtype=jnp.int32) % 2
    return jax.vmap(one_row)(keys, parities).astype(jnp.int32)


def levels(own_key, extent, pieces, smallest, largest):
    def one(dim, parts):
        steps = jax.random.uniform(jax.random.fold_in(jax.random.fold_in(own_key, 6), dim), (parts,), jnp.float32, smallest / len(pieces), largest / len(pieces))
        return jnp.repeat(jnp.exp(steps), extent[dim] // parts).reshape((-1,) + (1,) * (len(extent) - dim - 1))

    level = one(*pieces[0])
    for cut in pieces[1:]:
        level = level * one(*cut)
    return level


def centred(rng, extent, width, reach, shards=(), held_as=jnp.bfloat16):
    array = width * jax.random.normal(rng, extent, jnp.float32)
    if shards:
        array = array * levels(rng, extent, shards, -0.22, 0.18)
    return jnp.clip(array, -reach, reach).astype(held_as)


def setup_inputs(seed: int = 0) -> dict:
    key_list = jax.random.split(jax.random.key(seed), 12)
    rhs_leaves = centred(key_list[0], (LEAVES, W, NRHS), 1.0, 6.0, ((0, 16), (2, 8)))
    rhs_roots = centred(key_list[1], (ROOTS, W, NRHS), 1.0, 6.0, ((0, 16), (2, 8)))
    rhs_seps = centred(key_list[2], (ROOTS, W, NRHS), 1.0, 6.0, ((0, 16), (2, 8)))
    above_solution = centred(key_list[3], (W, NRHS), 1.0, 6.0, ((1, 8),))
    leaf_inverse = centred(key_list[4], (LEAVES, W, W), W ** -0.5, 0.375, ((0, 16), (1, 8)))
    leaf_update = centred(key_list[5], (LEAVES, K, W), (NS * K) ** -0.5, 0.109375, ((0, 16), (1, 8)))
    leaf_rows = draw_leaf_rows(jax.random.fold_in(key_list[11], 71), 0)
    root_inverse = centred(key_list[7], (ROOTS, W, W), W ** -0.5, 0.375, ((0, 16), (1, 8)))
    root_coupling = centred(key_list[8], (ROOTS, W, W), (2 * W) ** -0.5, 0.25, ((0, 16), (1, 8)))
    sep_inverse = centred(key_list[9], (ROOTS, W, W), W ** -0.5, 0.375, ((0, 16), (1, 8)))
    sep_coupling = centred(key_list[10], (ROOTS, W, W), (2 * W) ** -0.5, 0.25, ((0, 16), (1, 8)))
    return {"rhs_leaves": rhs_leaves, "rhs_roots": rhs_roots, "rhs_seps": rhs_seps, "above_solution": above_solution, "leaf_inverse": leaf_inverse, "leaf_update": leaf_update, "leaf_rows": leaf_rows, "root_inverse": root_inverse, "root_coupling": root_coupling, "sep_inverse": sep_inverse, "sep_coupling": sep_coupling}


def batched(left, right):
    return jnp.einsum("nab,nbr->nar", left.astype(jnp.float32), right.astype(jnp.float32))


def batched_transposed(left, right):
    return jnp.einsum("nab,nar->nbr", left.astype(jnp.float32), right.astype(jnp.float32))


def node_levels(count):
    position = np.arange(count) + 1
    level = np.ones(count, dtype=np.int32)
    for bit in range(1, count.bit_length()):
        level = level + (position % (2 ** bit) == 0).astype(np.int32)
    return level


def solve_top(rhs_seps, root_flow, sep_inverse, sep_coupling, above_solution):
    count = rhs_seps.shape[0]
    depth = count.bit_length() - 1
    level = node_levels(count)
    values = jnp.zeros((count + 1,) + rhs_seps.shape[1:], jnp.bfloat16)
    flows = jnp.zeros_like(values)
    for height in range(1, depth + 2):
        nodes = np.arange(count)[level == height].astype(np.int32)
        if height == 1:
            inflow = root_flow[nodes].astype(jnp.float32) + root_flow[nodes + 1].astype(jnp.float32)
        else:
            stride = 2 ** (height - 2)
            upper = np.where(nodes + stride < count, nodes + stride, count).astype(np.int32)
            inflow = flows[nodes - stride].astype(jnp.float32) + flows[upper].astype(jnp.float32)
        assembled = (rhs_seps[nodes].astype(jnp.float32) - inflow).astype(jnp.bfloat16)
        solved = batched(sep_inverse[nodes], assembled).astype(jnp.bfloat16)
        values = values.at[nodes].set(solved)
        flows = flows.at[nodes].set(batched(sep_coupling[nodes], solved).astype(jnp.bfloat16))
    answers = jnp.zeros_like(values).at[count].set(above_solution)
    for height in range(depth + 1, 0, -1):
        nodes = np.arange(count)[level == height].astype(np.int32)
        if height == depth + 1:
            parents = (nodes * 0 + count).astype(np.int32)
        else:
            stride = 2 ** (height - 1)
            order = (nodes + 1 - stride) // (2 * stride)
            parents = np.where(order % 2 == 0, nodes + stride, nodes - stride).astype(np.int32)
        reduced = (values[nodes].astype(jnp.float32) - batched_transposed(sep_coupling[nodes], answers[parents])).astype(jnp.bfloat16)
        answers = answers.at[nodes].set(batched_transposed(sep_inverse[nodes], reduced).astype(jnp.bfloat16))
    return values[:count], answers[:count]


def reference(rhs_leaves, rhs_roots, rhs_seps, above_solution, leaf_inverse, leaf_update, leaf_rows, root_inverse, root_coupling, sep_inverse, sep_coupling):
    blocks_inverse = leaf_inverse.reshape(ROOTS, NS, W, W)
    blocks_update = leaf_update.reshape(ROOTS, NS, K, W)
    blocks_rows = leaf_rows.reshape(ROOTS, NS, K)

    def leaf_forward(block):
        rhs, inverse, update, rows = block
        solved = batched(inverse, rhs).astype(jnp.bfloat16)
        sent = batched(update, solved).astype(jnp.bfloat16)
        total = jnp.zeros((W, NRHS), jnp.float32).at[rows.reshape(-1)].add(sent.reshape(NS * K, NRHS).astype(jnp.float32))
        return solved, total

    solved_leaves, root_sum = lax.map(leaf_forward, (rhs_leaves.reshape(ROOTS, NS, W, NRHS), blocks_inverse, blocks_update, blocks_rows))
    root_rhs = (rhs_roots.astype(jnp.float32) - root_sum).astype(jnp.bfloat16)
    solved_roots = batched(root_inverse, root_rhs).astype(jnp.bfloat16)
    root_flow = batched(root_coupling, solved_roots).astype(jnp.bfloat16)
    solved_seps, solution_seps = solve_top(rhs_seps, root_flow, sep_inverse, sep_coupling, above_solution)
    parents = (np.arange(ROOTS) // 2 * 2).astype(np.int32)
    root_reduced = (solved_roots.astype(jnp.float32) - batched_transposed(root_coupling, solution_seps[parents])).astype(jnp.bfloat16)
    solution_roots = batched_transposed(root_inverse, root_reduced).astype(jnp.bfloat16)

    def leaf_backward(block):
        solved, top, inverse, update, rows = block
        picked = top[rows]
        reduced = (solved.astype(jnp.float32) - batched_transposed(update, picked)).astype(jnp.bfloat16)
        return batched_transposed(inverse, reduced).astype(jnp.bfloat16)

    solution_leaves = lax.map(leaf_backward, (solved_leaves, solution_roots, blocks_inverse, blocks_update, blocks_rows))
    return solution_leaves.reshape(LEAVES, W, NRHS), solution_roots, solution_seps
```

```python
import functools

import jax
import jax.numpy as jnp
from jax import lax
from jax.experimental import pallas as pl
from jax.experimental.pallas import tpu as pltpu
from jax.sharding import PartitionSpec as P

BF = jnp.bfloat16
F32 = jnp.float32


def mm(a, b):
    return jnp.dot(a, b, preferred_element_type=F32)


def mmt(a, b):
    return lax.dot_general(a, b, (((0,), (0,)), ((), ())), preferred_element_type=F32)


def sub(rhs, inflow):
    return (rhs.astype(F32) - inflow).astype(BF)


def f32sum(a, b):
    return a.astype(F32) + b.astype(F32)


def y_shift(s):
    return [(x * 4 + y, x * 4 + (y + s) % 4) for x in range(2) for y in range(4)]


def z_shift(s):
    return [
        (x * 8 + z * 2 + c, x * 8 + ((z + s) % 4) * 2 + c)
        for x in range(2)
        for z in range(4)
        for c in range(2)
    ]


X_LO = [(i, (i + 4) % 8) for i in range(8)]
X_HI = [(i, (i + 8) % 16) for i in range(16)]
CORE = [(i, i ^ 1) for i in range(16)]


def up(v):
    return lax.ppermute(v, "load", y_shift(1))


def down(v):
    return lax.ppermute(v, "load", y_shift(3))


def across(v):
    return lax.ppermute(v, "load", X_LO)


def other_core(v):
    return lax.ppermute(v, "leaf", CORE)


def other_half(v):
    return lax.ppermute(v, "leaf", X_HI)


def along_z(v, s):
    return lax.ppermute(v, "leaf", z_shift(s))


VMEM = pl.BlockSpec(memory_space=pltpu.VMEM)
SMEM = pl.BlockSpec(memory_space=pltpu.SMEM)


def spec(block, index):
    return pl.BlockSpec(block, index)


def shape(dims, dtype=BF):
    return jax.ShapeDtypeStruct(dims, dtype)


def small_kernel(offs, *refs):
    blocks, (root_ref, sep_ref, full) = refs[:8], refs[8:]
    for k, block in enumerate(blocks):
        rows = block[...].reshape(144, 256)
        at = pl.multiple_of(offs[k] * 32, 32)
        for m in range(4):
            full[m, pl.ds(at, 32), :] = rows[32 * m : 32 * m + 32]
    for m, out in ((0, root_ref), (2, sep_ref)):
        inv, cpl = full[m], full[m + 1]
        out[0] = mm(cpl, inv).astype(BF)
        out[1] = mmt(inv, inv).astype(BF)


def small_blocks(offs, blocks):
    head = spec((3, 48, 256), lambda i: (0, 0, 0))
    return pl.pallas_call(
        small_kernel,
        grid=(1,),
        in_specs=[SMEM] + [head] * 8,
        out_specs=[spec((2, 256, 256), lambda i: (0, 0, 0))] * 2,
        out_shape=[shape((2, 256, 256))] * 2,
        scratch_shapes=[pltpu.VMEM((4, 256, 256), BF)],
        cost_estimate=pl.CostEstimate(flops=4 * 2**25, bytes_accessed=2**20, transcendentals=0),
    )(offs, *blocks)


STEP = 4


def forward_kernel(split, offs, *refs):
    blocks = refs[:9]
    rhs, rows, before, m_ref, inv_ref, total, inv, upd = refs[9:]
    step = pl.program_id(0)

    @pl.when(step == 0)
    def _():
        total[...] = before[...]

    at = [offs[k] for k in range(8)]

    def place(i, k, rows48):
        inv[i, pl.ds(pl.multiple_of(at[k] * 32, 32), 32), :] = rows48[:32]
        upd[i, pl.ds(pl.multiple_of(at[k] * 16, 16), 16), :] = rows48[32:]

    for i in range(STEP):
        for k in range(7):
            place(i, k, blocks[k][i])

    @pl.when(step < split)
    def _():
        for i in range(STEP):
            place(i, 7, blocks[7][i])

    @pl.when(step >= split)
    def _():
        for i in range(STEP):
            place(i, 7, blocks[8][i])

    inv_ref[...] = inv[...]
    parts = []
    for i in range(STEP):
        s = mm(upd[i], inv[i]).astype(BF)
        hot = (lax.broadcasted_iota(jnp.int32, (256, 128), 0) == rows[i]).astype(BF)
        m = mm(hot, s).astype(BF)
        m_ref[i] = m
        parts.append(m)
    total[...] += mm(jnp.concatenate(parts, axis=1), rhs[...].reshape(STEP * 256, 512))


def leaves_forward(offs, blocks, skips, rest, rhs, first, rows, before):
    count = 12
    split = 8 // STEP
    specs = []
    for skip in skips:
        specs.append(skip)
    lead = [
        spec((pl.Element(STEP), pl.Element(48), pl.Element(256)), lambda i, s=s: (i * STEP + s, 0, 0))
        for s in skips
    ]
    lead.append(spec((STEP, 48, 256), lambda i: (jnp.minimum(i, split - 1), 0, 0)))
    lead.append(spec((STEP, 48, 256), lambda i: (jnp.maximum(i - split, 0), 0, 0)))
    return pl.pallas_call(
        functools.partial(forward_kernel, split),
        grid=(count // STEP,),
        in_specs=[SMEM]
        + lead
        + [
            spec((STEP, 256, 512), lambda i: (i + first // STEP, 0, 0)),
            spec((STEP, 1, 128), lambda i: (i + first // STEP, 0, 0)),
            spec((256, 512), lambda i: (0, 0)),
        ],
        out_specs=[
            spec((STEP, 256, 256), lambda i: (i, 0, 0)),
            spec((STEP, 256, 256), lambda i: (i, 0, 0)),
            spec((256, 512), lambda i: (0, 0)),
        ],
        out_shape=[shape((count, 256, 256)), shape((count, 256, 256)), shape((256, 512), F32)],
        scratch_shapes=[pltpu.VMEM((STEP, 256, 256), BF), pltpu.VMEM((STEP, 128, 256), BF)],
        cost_estimate=pl.CostEstimate(flops=2**31, bytes_accessed=12 * 2**20, transcendentals=0),
    )(offs, *blocks, *rest, rhs, rows, before)


def prepare_kernel(inv, m, out):
    for i in range(STEP):
        out[i, :, :256] = mmt(inv[i], inv[i]).astype(BF)
        out[i, :, 256:] = -(m[i].T)


def prepare(inv, m):
    count = inv.shape[0]
    block = spec((STEP, 256, 256), lambda i: (i, 0, 0))
    return pl.pallas_call(
        prepare_kernel,
        grid=(count // STEP,),
        in_specs=[block, block],
        out_specs=spec((STEP, 256, 512), lambda i: (i, 0, 0)),
        out_shape=shape((count, 256, 512)),
        cost_estimate=pl.CostEstimate(flops=2**29, bytes_accessed=6 * 2**20, transcendentals=0),
    )(inv, m)


def root_kernel(place, rhs, total, mats, r_ref, keep, send):
    r = sub(rhs[0], total[...])
    r_ref[...] = r
    flow = mm(mats[0], r).astype(BF)

    @pl.when(place[0] == 0)
    def _():
        keep[...] = flow[:, :256]
        send[...] = flow[:, 256:]

    @pl.when(place[0] == 1)
    def _():
        keep[...] = flow[:, 256:]
        send[...] = flow[:, :256]


def level_one_kernel(rhs, mine, theirs, mats, r_ref, flow):
    r = sub(rhs[...], f32sum(mine[...], theirs[...]))
    r_ref[...] = r
    flow[...] = mm(mats[0], r).astype(BF)


def middle_kernel(place, f0, f1, f2, f3, rhs, a, r_out, flow, flows):
    z = place[1]
    for k, f in enumerate((f0, f1, f2, f3)):
        flows[lax.rem(z - k + 4, 4)] = f[...]
    i0, i1, i2 = place[2], place[3], place[4]
    r0 = sub(rhs[i0], f32sum(flows[0], flows[1]))
    r2 = sub(rhs[i2], f32sum(flows[2], flows[3]))
    g0 = mm(a[i0], r0).astype(BF)
    g2 = mm(a[i2], r2).astype(BF)
    r1 = sub(rhs[i1], f32sum(g0, g2))
    flow[...] = mm(a[i1], r1).astype(BF)
    r_out[0] = r0
    r_out[1] = r1
    r_out[2] = r2


def top_kernel(place, mine, theirs, rhs, a, g, rs, r_even, even, above, out, ans):
    i0, i1, i2, i3 = place[2], place[3], place[4], place[5]
    i7, i15 = place[6], place[7]
    r7 = sub(rhs[i7], f32sum(mine[...], theirs[...]))
    f7 = mm(a[i7], r7).astype(BF)
    r15 = sub(rhs[i15], f7.astype(F32))
    x15 = (mm(g[i15], r15) - mmt(a[i15], above[...])).astype(BF)
    x7 = (mm(g[i7], r7) - mmt(a[i7], x15)).astype(BF)
    x1 = (mm(g[i1], rs[1]) - mmt(a[i1], x7)).astype(BF)
    x0 = (mm(g[i0], rs[0]) - mmt(a[i0], x1)).astype(BF)
    x2 = (mm(g[i2], rs[2]) - mmt(a[i2], x1)).astype(BF)
    ans[0] = x0
    ans[1] = x1
    ans[2] = x2
    ans[3] = jnp.where(place[8] == 0, x7, x15)
    parent = ans[place[9]]
    out[0] = (mm(even[1], r_even[...]) - mmt(even[0], parent)).astype(BF)
    out[1] = ans[place[1]]


def call(kernel, outs, *args, scratch=(), flops=2**26):
    specs = [SMEM if a.dtype == jnp.int32 else VMEM for a in args]
    return pl.pallas_call(
        kernel,
        in_specs=specs,
        out_specs=[VMEM] * len(outs),
        out_shape=[shape(o) for o in outs],
        scratch_shapes=list(scratch),
        cost_estimate=pl.CostEstimate(flops=flops, bytes_accessed=2**20, transcendentals=0),
    )(*args)


def backward_kernel(place, r, mats, mine, theirs, rhs, gm, leaf_out, root_out, sep_out, answer):
    @pl.when(pl.program_id(0) == 0)
    def _():
        core = place[0]
        first = jnp.where(core == 0, mine[...], theirs[...])
        second = jnp.where(core == 0, theirs[...], mine[...])
        parent = jnp.concatenate([first[0], second[0]], axis=1)
        value = (mm(mats[1], r[...]) - mmt(mats[0], parent)).astype(BF)
        answer[...] = value
        root_out[0] = value
        odd = jnp.concatenate([first[1], second[1]], axis=1)
        sep_out[0] = jnp.where(core == 0, parent, odd)

    for i in range(rhs.shape[0]):
        leaf_out[i] = (mm(gm[i, :, :256], rhs[i]) + mm(gm[i, :, 256:], answer[...])).astype(BF)


def backward(place, r, mats, mine, theirs, rhs, gm):
    step = 4
    whole = lambda *dims: spec(dims, lambda i: (0,) * len(dims))
    return pl.pallas_call(
        backward_kernel,
        grid=(24 // step,),
        in_specs=[
            SMEM,
            whole(256, 512),
            whole(2, 256, 256),
            whole(2, 256, 256),
            whole(2, 256, 256),
            spec((step, 256, 512), lambda i: (i, 0, 0)),
            spec((step, 256, 512), lambda i: (i, 0, 0)),
        ],
        out_specs=[
            spec((step, 256, 512), lambda i: (i, 0, 0)),
            whole(1, 256, 512),
            whole(1, 256, 512),
        ],
        out_shape=[shape((24, 256, 512)), shape((1, 256, 512)), shape((1, 256, 512))],
        scratch_shapes=[pltpu.VMEM((256, 512), BF)],
        cost_estimate=pl.CostEstimate(flops=2**32, bytes_accessed=18 * 2**20, transcendentals=0),
    )(place, r, mats, mine, theirs, rhs, gm)


def local(
    rhs_leaves,
    rhs_roots,
    rhs_seps,
    above_solution,
    leaf_inverse,
    leaf_update,
    leaf_rows,
    root_inverse,
    root_coupling,
    sep_inverse,
    sep_coupling,
):
    position = lax.axis_index("leaf")
    core, z, x_hi = position % 2, (position // 2) % 4, position // 8
    load = lax.axis_index("load")
    x, y = load // 4, load % 4
    rel = [(x, y), (x, y + 3), (x, y + 1), (x, y + 2), (1 - x, y), (1 - x, y + 3), (1 - x, y + 1), (1 - x, y + 2)]
    offs = jnp.stack([a * 4 + b % 4 for a, b in rel]).astype(jnp.int32)
    index = [(z + 4 - j) % 4 for j in range(4)]
    i7 = jnp.where(x_hi == 0, index[3], 4)
    i15 = jnp.where(x_hi == 0, 4, index[3])
    place = jnp.stack([core, z, *index, i7, i15, x_hi, (z // 2) * 2]).astype(jnp.int32)

    pad = jnp.zeros((16, 256), BF)
    small = jnp.concatenate(
        [root_inverse[0], root_coupling[0], sep_inverse[0], sep_coupling[0], pad], axis=0
    ).reshape(3, 48, 256)
    both = jnp.concatenate([leaf_inverse, leaf_update], axis=1)
    w1 = jnp.concatenate([small, both[:12]], axis=0)
    w2 = both[12:]
    a1, b1, c1 = up(w1), down(w1), across(w1)
    a2, b2, c2 = up(w2), down(w2), across(w2)
    d1, bm1, am1 = up(a1), down(c1), across(a1)
    e2, am2, bm2 = down(b2), up(c2), across(b2)
    s_opp = across(d1[:3])
    g1, k1 = up(am1[3:11]), across(d1[11:])
    g2, k2 = down(bm2[:8]), across(e2[8:])
    blocks1 = [w1, a1, b1, d1, c1, am1, bm1]
    blocks2 = [w2, a2, b2, e2, c2, am2, bm2]

    own_half = lax.dynamic_slice(rhs_seps[0], (0, core * 256), (256, 256))
    far_half = lax.dynamic_slice(rhs_seps[0], (0, (1 - core) * 256), (256, 256))
    got = other_core(far_half)
    rhs_even = jnp.where(core == 0, own_half, got)
    rhs_odd = jnp.where(core == 0, got, own_half)
    rhs_z = [rhs_odd] + [along_z(rhs_odd, s) for s in (1, 2, 3)]
    rhs_z = jnp.stack(rhs_z)
    rhs_hi = other_half(lax.dynamic_index_in_dim(rhs_z, index[3], 0, False))
    rhs_tree = jnp.concatenate([rhs_z, rhs_hi[None]], axis=0)
    above = lax.dynamic_slice(above_solution, (0, core * 256), (256, 256))

    root_mats, sep_mats = small_blocks(offs, blocks1 + [s_opp])
    sep_got = other_core(sep_mats)
    even = jnp.where(core == 0, sep_mats, sep_got)
    odd = jnp.where(core == 0, sep_got[0], sep_mats[1])
    odd_z = jnp.stack([odd] + [along_z(odd, s) for s in (1, 2, 3)])
    odd_hi = other_half(lax.dynamic_index_in_dim(odd_z, index[3], 0, False))
    mine = jnp.concatenate([odd_z, odd_hi[None]], axis=0)
    theirs = other_core(mine)
    mats_a = jnp.where(core == 0, mine, theirs)
    mats_g = jnp.where(core == 0, theirs, mine)

    rows = leaf_rows.reshape(24, 1, 128)
    nothing = jnp.zeros((256, 512), F32)
    m1, inv1, total = leaves_forward(
        offs, blocks1, [3] * 7, [g1, k1], rhs_leaves, 0, rows, nothing
    )
    m2, inv2, total = leaves_forward(
        offs, blocks2, [0] * 7, [g2, k2], rhs_leaves, 12, rows, total
    )
    gm = jnp.concatenate([prepare(inv1, m1), prepare(inv2, m2)], axis=0)

    r_root, keep, send = call(
        root_kernel, [(256, 512), (256, 256), (256, 256)], place, rhs_roots, total, root_mats
    )
    r_even, flow = call(
        level_one_kernel, [(256, 256), (256, 256)], rhs_even, keep, other_core(send), even
    )
    flows = [flow] + [along_z(flow, s) for s in (1, 2, 3)]
    rs, flow = call(
        middle_kernel,
        [(3, 256, 256), (256, 256)],
        place,
        *flows,
        rhs_tree,
        mats_a,
        scratch=[pltpu.VMEM((4, 256, 256), BF)],
    )
    (answers,) = call(
        top_kernel,
        [(2, 256, 256)],
        place,
        flow,
        other_half(flow),
        rhs_tree,
        mats_a,
        mats_g,
        rs,
        r_even,
        even,
        above,
        scratch=[pltpu.VMEM((4, 256, 256), BF)],
    )
    leaf, root, sep = backward(
        place, r_root, root_mats, answers, other_core(answers), rhs_leaves, gm
    )
    return leaf, root, sep


def solution(mesh):
    rows = P("leaf", "load", None)
    columns = P("leaf", None, "load")
    in_specs = (columns, columns, columns, P(None, "load"), rows, rows, P("leaf", None)) + (rows,) * 4
    return jax.shard_map(
        local, mesh=mesh, in_specs=in_specs, out_specs=(columns,) * 3, check_vma=False
    )
```

```python
import functools

import jax
import jax.numpy as jnp
from jax import lax
from jax.experimental import pallas as pl
from jax.experimental.pallas import tpu as pltpu
from jax.sharding import PartitionSpec as P

BF = jnp.bfloat16
F32 = jnp.float32

ODD = range(1, 16, 2)


def mm(a, b):
    return jnp.dot(a, b, preferred_element_type=F32)


def mmt(a, b):
    return lax.dot_general(a, b, (((0,), (0,)), ((), ())), preferred_element_type=F32)


def sub(rhs, inflow):
    return (rhs.astype(F32) - inflow).astype(BF)


def f32sum(a, b):
    return a.astype(F32) + b.astype(F32)


def y_shift(s):
    return [(x * 4 + y, x * 4 + (y + s) % 4) for x in range(2) for y in range(4)]


def z_shift(s, places):
    return [(x * 8 + z * 2 + 1, x * 8 + ((z + s) % 4) * 2 + 1) for x in range(2) for z in places]


X_LO = [(i, (i + 4) % 8) for i in range(8)]
X_HI = [(p, (p + 8) % 16) for p in ODD]
PAIR = [(p, p ^ 2) for p in ODD]
MIRROR = [(p, (p // 8) * 8 + (3 - (p // 2) % 4) * 2 + 1) for p in ODD]
TO_ODD = [(p - 1, p) for p in ODD]
TO_EVEN = [(p, p - 1) for p in ODD]


def up(v):
    return lax.ppermute(v, "load", y_shift(1))


def down(v):
    return lax.ppermute(v, "load", y_shift(3))


def across(v):
    return lax.ppermute(v, "load", X_LO)


def among(v, pairs):
    return lax.ppermute(v, "leaf", pairs)


def shape(dims, dtype=BF):
    return jax.ShapeDtypeStruct(dims, dtype)


VMEM = pl.BlockSpec(memory_space=pltpu.VMEM)
ANY = pl.BlockSpec(memory_space=pl.ANY)


def call(kernel, outs, *args, scratch=(), flops=2**26, limit=8, size=2**20, **specs):
    return pl.pallas_call(
        kernel,
        in_specs=specs.get("in_specs", [VMEM] * len(args)),
        out_specs=specs.get("out_specs", [VMEM] * len(outs)),
        out_shape=[o if isinstance(o, jax.ShapeDtypeStruct) else shape(o) for o in outs],
        scratch_shapes=list(scratch),
        compiler_params=pltpu.CompilerParams(vmem_limit_bytes=limit * 2**20),
        cost_estimate=pl.CostEstimate(flops=flops, bytes_accessed=size, transcendentals=0),
    )(*args)


ORIGINS = [(0, 0), (0, 3), (0, 1), (1, 0), (0, 2), (1, 3), (1, 1), (1, 2)]


def origin(slot):
    load = lax.axis_index("load")
    dx, dy = ORIGINS[slot]
    return lax.rem(load // 4 + dx, 2) * 4 + lax.rem(load + dy, 4)


def leaf_place():
    position = lax.axis_index("leaf")
    return lax.rem(position, 2), lax.rem(position // 2, 4), position // 8


def pack_kernel(*refs):
    smalls, (inv, upd, out, small, sems) = refs[:4], refs[4:]
    pairs = [(inv, out.at[:, pl.ds(0, 32)]), (upd, out.at[:, pl.ds(32, 16)])]
    for n, ref in enumerate(smalls):
        for to in range(8):
            pairs.append((ref.at[0], small.at[to, pl.ds(32 * n, 32)]))
    copies = [pltpu.make_async_copy(a, b, sems.at[n]) for n, (a, b) in enumerate(pairs)]
    for copy in copies:
        copy.start()
    for copy in copies:
        copy.wait()


def small_kernel(rows, rhs, root_ref, pack):
    full = [
        jnp.concatenate([rows[d, 32 * m : 32 * m + 32, :] for d in range(8)], axis=0)
        for m in range(4)
    ]
    for m, out in ((0, root_ref), (2, pack)):
        inv, cpl = full[m], full[m + 1]
        out[0] = mm(cpl, inv).astype(BF)
        out[1] = mmt(inv, inv).astype(BF)
    pack[2] = rhs[0, :, :256]
    pack[3] = rhs[0, :, 256:]


HALF = 12


def forward_kernel(*refs):
    common, last = refs[:7], refs[7:9]
    rhs, rows, m_ref, inv, total, upd = refs[9:]
    for n in range(2):
        first = n * HALF
        for slot in range(8):
            if slot < 7:
                rows48 = common[slot][pl.ds(first, HALF)]
            else:
                rows48 = last[n][...]
            at = origin(slot)
            inv[pl.ds(first, HALF), pl.ds(pl.multiple_of(at * 32, 32), 32), :] = rows48[:, :32]
            upd[:, pl.ds(pl.multiple_of(at * 16, 16), 16), :] = rows48[:, 32:]
        flows = [mm(upd[i], inv[first + i]).astype(BF) for i in range(HALF)]
        parts = []
        for i in range(HALF):
            hot = lax.broadcasted_iota(jnp.int32, (256, 128), 0) == rows[first + i]
            m = mm(hot.astype(BF), flows[i]).astype(BF)
            m_ref[first + i] = m
            parts.append(m)
        new = mm(
            jnp.concatenate(parts, axis=1), rhs[pl.ds(first, HALF)].reshape(HALF * 256, 512)
        )
        total[...] = new if n == 0 else total[...] + new


def leaves_forward(blocks, rhs, rows):
    return call(
        forward_kernel,
        [(24, 256, 256), (24, 256, 256), shape((256, 512), F32)],
        *blocks,
        rhs,
        rows,
        scratch=[
            pltpu.VMEM((HALF, 128, 256), BF),
        ],
        flops=2**32,
        size=2**24,
        limit=16,
    )


def prepare_kernel(first, inv, m, rhs, base, mt):
    count = base.shape[0]
    squares = [mmt(inv[first + i], inv[first + i]).astype(BF) for i in range(count)]
    for i in range(count):
        mt[i] = -(m[first + i].T)
    for i in range(count):
        base[i] = mm(squares[i], rhs[first + i]).astype(BF)


def prepare(first, count, inv, m, rhs):
    return call(
        functools.partial(prepare_kernel, first),
        [(count, 256, 512), (count, 256, 256)],
        inv,
        m,
        rhs,
        flops=count * 2**27,
    )


def root_kernel(rhs, total, mats, r_ref, flow):
    r = sub(rhs[0], total[...])
    r_ref[...] = r
    flow[...] = mm(mats[0], r).astype(BF)


def halves(pack):
    return jnp.concatenate([pack[2], pack[3]], axis=1)


def first_kernel(pack, mine, theirs, r_ref, flow, mats):
    r = sub(halves(pack), f32sum(mine[...], theirs[...]))
    r_ref[...] = r
    flow[...] = mm(pack[0], r).astype(BF)
    mats[0] = pack[0].T
    mats[1] = pack[1]


def middle_kernel(*refs):
    packs, flows, (r_ref, flow, mats) = refs[:4], refs[4:8], refs[8:]
    z = leaf_place()[1]
    for k in range(4):

        @pl.when(z == k)
        def _():
            p = [packs[(k - j) % 4] for j in range(4)]
            f = [flows[(k - j) % 4] for j in range(4)]
            r = [None] * 3
            out = [None] * 3
            for j in (0, 2):
                r[j] = sub(halves(p[j]), f32sum(f[j][...], f[j + 1][...]))
                out[j] = mm(p[j][0], r[j]).astype(BF)
            r[1] = sub(halves(p[1]), f32sum(out[0], out[2]))
            flow[...] = mm(p[1][0], r[1]).astype(BF)
            for n, j in enumerate((k // 2 * 2, 1)):
                r_ref[n] = r[j]
                mats[n, 0] = p[j][0].T
                mats[n, 1] = p[j][1]


def choose_kernel(own, s1, s2, s3, out):
    z = leaf_place()[1]
    for k, ref in enumerate((s1, s2, s3, own)):

        @pl.when(z == k)
        def _():
            out[...] = ref[...]


def top_kernel(mine, theirs, top, far, t0, t, r0, r, above, even, odd, p3, p4):
    _, z, x_hi = leaf_place()

    @pl.when(x_hi == 0)
    def _():
        p3[...] = top[...]
        p4[...] = far[...]

    @pl.when(x_hi == 1)
    def _():
        p3[...] = far[...]
        p4[...] = top[...]

    r3 = sub(halves(p3), f32sum(mine[...], theirs[...]))
    r4 = sub(halves(p4), mm(p3[0], r3).astype(BF).astype(F32))
    x4 = (mm(p4[1], r4) - mmt(p4[0], above[...])).astype(BF)
    x3 = (mm(p3[1], r3) - mmt(p3[0], x4)).astype(BF)
    x2 = (mm(t[1, 1], r[1]) - mm(t[1, 0], x3)).astype(BF)
    x1 = (mm(t[0, 1], r[0]) - mm(t[0, 0], x2)).astype(BF)
    even[...] = (mm(t0[1], r0[...]) - mm(t0[0], x1)).astype(BF)

    @pl.when(z % 2 == 0)
    def _():
        odd[...] = x1

    @pl.when(z == 1)
    def _():
        odd[...] = x2

    @pl.when(z == 3)
    def _():
        odd[...] = jnp.where(x_hi == 0, x3, x4)


PIECE = 2


def backward_kernel(parts, r, mats, even, odd, got, *refs):
    bases, mts = refs[:parts], refs[parts : 2 * parts]
    leaf_out, root_out, sep_out, small, held, sems, small_sems = refs[2 * parts :]
    core = leaf_place()[0]
    parent = jnp.where(core == 0, got[...], even[...])
    small[0] = (mm(mats[1], r[...]) - mmt(mats[0], parent)).astype(BF)
    small[1] = jnp.where(core == 0, got[...], odd[...])
    copies = [
        pltpu.make_async_copy(small.at[n], ref.at[0], small_sems.at[n])
        for n, ref in enumerate((root_out, sep_out))
    ]
    for copy in copies:
        copy.start()
    count = 24 // PIECE
    for step in range(count):
        part, at = divmod(step, count // parts)
        here = pl.ds(at * PIECE, PIECE)
        moved = mm(mts[part][here].reshape(PIECE * 256, 256), small[0])
        held[step] = (bases[part][here].astype(F32) + moved.reshape(PIECE, 256, 512)).astype(BF)
        copy = pltpu.make_async_copy(
            held.at[step], leaf_out.at[pl.ds(step * PIECE, PIECE)], sems.at[step]
        )
        copy.start()
        copies.append(copy)
    for copy in copies:
        copy.wait()


def backward(r, mats, even, odd, got, bases, mts):
    return call(
        functools.partial(backward_kernel, len(bases)),
        [(24, 256, 512), (1, 256, 512), (1, 256, 512)],
        r,
        mats,
        even,
        odd,
        got,
        *bases,
        *mts,
        scratch=[
            pltpu.VMEM((2, 256, 512), BF),
            pltpu.VMEM((24 // PIECE, PIECE, 256, 512), BF),
            pltpu.SemaphoreType.DMA((24 // PIECE,)),
            pltpu.SemaphoreType.DMA((2,)),
        ],
        out_specs=[ANY] * 3,
        flops=2**31,
        size=2**24,
        limit=14,
    )


def local(
    rhs_leaves,
    rhs_roots,
    rhs_seps,
    above_solution,
    leaf_inverse,
    leaf_update,
    leaf_rows,
    root_inverse,
    root_coupling,
    sep_inverse,
    sep_coupling,
):
    w, small = call(
        pack_kernel,
        [(24, 48, 256), (8, 128, 256)],
        root_inverse,
        root_coupling,
        sep_inverse,
        sep_coupling,
        leaf_inverse,
        leaf_update,
        scratch=[pltpu.SemaphoreType.DMA((34,))],
        limit=56,
        in_specs=[ANY] * 6,
    )
    small = lax.all_to_all(small, "load", 0, 0)
    a, b, c, small = lax.optimization_barrier((up(w), down(w), across(w), small))
    d, e, f = lax.optimization_barrier((up(a), across(a), down(c)))
    blocks = (w, a, b, c, d, e, f)
    root_mats, pack = call(small_kernel, [(2, 256, 256), (4, 256, 256)], small, rhs_seps)

    over_z = lambda v: [among(v, z_shift(k, range(4))) for k in (1, 2, 3)]
    packs = over_z(pack)
    g, h = up(e[:HALF]), down(f[HALF:])
    (top,) = call(choose_kernel, [(4, 256, 256)], pack, *packs)
    far = among(top, X_HI)
    g, h, even_pack = lax.optimization_barrier((g, h, among(pack, TO_ODD)))

    m, inv, total = leaves_forward(
        (*blocks, g, h), rhs_leaves, leaf_rows.reshape(24, 1, 128)
    )

    r_root, flow = call(root_kernel, [(256, 512)] * 2, rhs_roots, total, root_mats)
    theirs, far = lax.optimization_barrier((among(flow, TO_ODD), far))
    r0, flow, t0 = call(
        first_kernel,
        [(256, 512), (256, 512), (2, 256, 256)],
        even_pack,
        flow,
        theirs,
    )
    flows = over_z(flow)
    held, flow = lax.optimization_barrier((inv, flow))
    parts = [prepare(8 * n, 8, held, m, rhs_leaves) for n in range(2)]
    flows, parts = lax.optimization_barrier((flows, parts))
    r, flow, t = call(
        middle_kernel,
        [(2, 256, 512), (256, 512), (2, 2, 256, 256)],
        pack,
        *packs,
        flow,
        *flows,
    )
    theirs = among(flow, X_HI)
    held, flow = lax.optimization_barrier((held, flow))
    parts.append(prepare(16, 8, held, m, rhs_leaves))
    theirs, parts = lax.optimization_barrier((theirs, parts))
    even, odd = call(
        top_kernel,
        [(256, 512)] * 2,
        flow,
        theirs,
        top,
        far,
        t0,
        t,
        r0,
        r,
        above_solution,
        scratch=[pltpu.VMEM((4, 256, 256), BF)] * 2,
    )
    return tuple(
        backward(
            r_root,
            root_mats,
            even,
            odd,
            among(even, TO_EVEN),
            [p[0] for p in parts],
            [p[1] for p in parts],
        )
    )


def solution(mesh):
    rows = P("leaf", "load", None)
    columns = P("leaf", None, "load")
    in_specs = (columns, columns, columns, P(None, "load"), rows, rows, P("leaf", None)) + (rows,) * 4
    return jax.shard_map(
        local, mesh=mesh, in_specs=in_specs, out_specs=(columns,) * 3, check_vma=False
    )
```

```python
import functools

import jax
import jax.numpy as jnp
from jax import lax
from jax.experimental import pallas as pl
from jax.experimental.pallas import tpu as pltpu
from jax.sharding import PartitionSpec as P

BF = jnp.bfloat16
F32 = jnp.float32


def mm(a, b):
    return jnp.dot(a, b, preferred_element_type=F32)


def mmt(a, b):
    return lax.dot_general(a, b, (((0,), (0,)), ((), ())), preferred_element_type=F32)


def sub(rhs, inflow):
    return (rhs.astype(F32) - inflow).astype(BF)


def f32sum(a, b):
    return a.astype(F32) + b.astype(F32)


def y_shift(s):
    return [(x * 4 + y, x * 4 + (y + s) % 4) for x in range(2) for y in range(4)]


def z_shift(s):
    return [
        (x * 8 + z * 2 + c, x * 8 + (z + s) % 4 * 2 + c)
        for x in range(2)
        for z in range(4)
        for c in range(2)
    ]


X_LO = [(p, (p + 4) % 8) for p in range(8)]
X_HI = [(p, (p + 8) % 16) for p in range(16)]
CORES = [(p, p ^ 1) for p in range(16)]


def up(v):
    return lax.ppermute(v, "load", y_shift(1))


def down(v):
    return lax.ppermute(v, "load", y_shift(3))


def across(v):
    return lax.ppermute(v, "load", X_LO)


def among(v, pairs):
    return lax.ppermute(v, "leaf", pairs)


def shape(dims, dtype=BF):
    return jax.ShapeDtypeStruct(dims, dtype)


VMEM = pl.BlockSpec(memory_space=pltpu.VMEM)
ANY = pl.BlockSpec(memory_space=pl.ANY)


def call(kernel, outs, *args, scratch=(), flops=2**26, limit=8, size=2**20, **specs):
    return pl.pallas_call(
        kernel,
        in_specs=specs.get("in_specs", [VMEM] * len(args)),
        out_specs=specs.get("out_specs", [VMEM] * len(outs)),
        out_shape=[o if isinstance(o, jax.ShapeDtypeStruct) else shape(o) for o in outs],
        scratch_shapes=list(scratch),
        compiler_params=pltpu.CompilerParams(vmem_limit_bytes=limit * 2**20),
        cost_estimate=pl.CostEstimate(flops=flops, bytes_accessed=size, transcendentals=0),
    )(*args)


ORIGINS = [(0, 0), (0, 3), (0, 1), (1, 0), (0, 2), (1, 3), (1, 1), (1, 2)]


def origin(slot):
    load = lax.axis_index("load")
    dx, dy = ORIGINS[slot]
    return lax.rem(load // 4 + dx, 2) * 4 + lax.rem(load + dy, 4)


def leaf_place():
    position = lax.axis_index("leaf")
    return lax.rem(position, 2), lax.rem(position // 2, 4), position // 8


def pack_kernel(*refs):
    smalls, (inv, upd, out, small, sems) = refs[:4], refs[4:]
    pairs = [(inv, out.at[:, pl.ds(0, 32)]), (upd, out.at[:, pl.ds(32, 16)])]
    for n, ref in enumerate(smalls):
        for to in range(8):
            pairs.append((ref.at[0], small.at[to, pl.ds(32 * n, 32)]))
    copies = [pltpu.make_async_copy(a, b, sems.at[n]) for n, (a, b) in enumerate(pairs)]
    for copy in copies:
        copy.start()
    for copy in copies:
        copy.wait()


def by_core(whole, keep, send):
    core = leaf_place()[0]
    for c in range(2):

        @pl.when(core == c)
        def _():
            keep[...] = whole[:, 256 * c : 256 * c + 256]
            send[...] = whole[:, 256 - 256 * c : 512 - 256 * c]


def small_kernel(rows, rhs, leaves, root_ref, keep, send):
    del leaves
    full = [
        jnp.concatenate([rows[d, 32 * m : 32 * m + 32, :] for d in range(8)], axis=0)
        for m in range(4)
    ]
    for m, outs in ((0, (root_ref,)), (2, (keep, send))):
        inv, cpl = full[m], full[m + 1]
        for n, value in enumerate((mm(cpl, inv).astype(BF), mmt(inv, inv).astype(BF))):
            for out in outs:
                out[n] = value
    by_core(rhs[0], keep.at[2], send.at[2])


def sides_kernel(own, got, even, odd, part):
    core = leaf_place()[0]
    for c, (a, b) in enumerate(((own, got), (got, own))):

        @pl.when(core == c)
        def _():
            even[...] = a[...]
            odd[...] = b[...]
            part[0] = b[c]
            part[1] = b[2]


def joined(core, mine, theirs):
    a = jnp.where(core == 0, mine[0], theirs[0])
    g = jnp.where(core == 0, theirs[0], mine[0])
    return a, g, mine[1]


def stage_kernel(*refs):
    n = len(refs) // 2
    ins, outs, sems = refs[:n], refs[n:-1], refs[-1]
    copies = [pltpu.make_async_copy(a, b, sems.at[n]) for n, (a, b) in enumerate(zip(ins, outs))]
    for copy in copies:
        copy.start()
    for copy in copies:
        copy.wait()


HALF = 12


def forward_kernel(*refs):
    common, last = refs[:7], refs[7:9]
    rhs, rows, m_ref, inv, total, upd = refs[9:]
    for n in range(2):
        first = n * HALF
        for slot in range(8):
            if slot < 7:
                rows48 = common[slot][pl.ds(first, HALF)]
            else:
                rows48 = last[n][...]
            at = origin(slot)
            inv[pl.ds(first, HALF), pl.ds(pl.multiple_of(at * 32, 32), 32), :] = rows48[:, :32]
            upd[:, pl.ds(pl.multiple_of(at * 16, 16), 16), :] = rows48[:, 32:]
        flows = [mm(upd[i], inv[first + i]).astype(BF) for i in range(HALF)]
        parts = []
        for i in range(HALF):
            hot = lax.broadcasted_iota(jnp.int32, (256, 128), 0) == rows[first + i]
            m = mm(hot.astype(BF), flows[i]).astype(BF)
            m_ref[first + i] = m
            parts.append(m)
        new = mm(
            jnp.concatenate(parts, axis=1), rhs[pl.ds(first, HALF)].reshape(HALF * 256, 512)
        )
        total[...] = new if n == 0 else total[...] + new


def leaves_forward(blocks, rhs, rows):
    return call(
        forward_kernel,
        [(24, 256, 256), (24, 256, 256), shape((256, 512), F32)],
        *blocks,
        rhs,
        rows,
        scratch=[
            pltpu.VMEM((HALF, 128, 256), BF),
        ],
        flops=2**20,
        size=2**24,
        limit=16,
    )


def prepare_kernel(first, inv, m, rhs, base, mt):
    count = base.shape[0]
    squares = [mmt(inv[first + i], inv[first + i]).astype(BF) for i in range(count)]
    for i in range(count):
        mt[i] = -(m[first + i].T)
    for i in range(count):
        base[i] = mm(squares[i], rhs[first + i]).astype(BF)


def prepare(first, count, inv, m, rhs):
    return call(
        functools.partial(prepare_kernel, first),
        [(count, 256, 512), (count, 256, 256)],
        inv,
        m,
        rhs,
        flops=count * 2**27,
    )


def root_kernel(rhs, total, mats, r_ref, keep, send):
    r = sub(rhs[0], total[...])
    r_ref[...] = r
    by_core(mm(mats[0], r).astype(BF), keep, send)


def first_kernel(pack, mine, theirs, r_ref, flow, mats):
    r = sub(pack[2], f32sum(mine[...], theirs[...]))
    r_ref[...] = r
    flow[...] = mm(pack[0], r).astype(BF)
    mats[0] = pack[0].T
    mats[1] = pack[1]


def middle_kernel(odd, *refs):
    mine, theirs, flows, (r_ref, flow, mats) = refs[:3], refs[3:6], refs[6:10], refs[10:]
    core, z, _ = leaf_place()
    for k in range(4):

        @pl.when(z == k)
        def _():
            p = []
            for j in range(4):
                n = (k - j) % 4
                p.append(joined(core, mine[n - 1], theirs[n - 1]) if n else odd)
            f = [flows[(k - j) % 4] for j in range(4)]
            r = [None] * 3
            out = [None] * 3
            for j in (0, 2):
                r[j] = sub(p[j][2], f32sum(f[j][...], f[j + 1][...]))
                out[j] = mm(p[j][0], r[j]).astype(BF)
            r[1] = sub(p[1][2], f32sum(out[0], out[2]))
            flow[...] = mm(p[1][0], r[1]).astype(BF)
            for n, j in enumerate((k // 2 * 2, 1)):
                r_ref[n] = r[j]
                mats[n, 0] = p[j][0].T
                mats[n, 1] = p[j][1]


def choose_kernel(odd, part, *refs):
    mine, theirs, (top, carried) = refs[:3], refs[3:6], refs[6:]
    core, z, _ = leaf_place()

    @pl.when(z == 3)
    def _():
        top[...] = odd[...]
        carried[...] = part[...]

    for k in range(3):

        @pl.when(z == k)
        def _():
            for n, value in enumerate(joined(core, mine[k], theirs[k])):
                top[n] = value
            carried[...] = mine[k][...]


def top_kernel(mine, theirs, top, far, far2, t0, t, r0, r, above, out, p3, p4):
    core, z, x_hi = leaf_place()
    above = above[:, pl.ds(pl.multiple_of(core * 256, 256), 256)]
    for h, (a, b) in enumerate(((p3, p4), (p4, p3))):

        @pl.when(x_hi == h)
        def _():
            a[...] = top[...]
            for n, value in enumerate(joined(core, far, far2)):
                b[n] = value

    r3 = sub(p3[2], f32sum(mine[...], theirs[...]))
    r4 = sub(p4[2], mm(p3[0], r3).astype(BF).astype(F32))
    x4 = (mm(p4[1], r4) - mmt(p4[0], above)).astype(BF)
    x3 = (mm(p3[1], r3) - mmt(p3[0], x4)).astype(BF)
    x2 = (mm(t[1, 1], r[1]) - mm(t[1, 0], x3)).astype(BF)
    x1 = (mm(t[0, 1], r[0]) - mm(t[0, 0], x2)).astype(BF)
    out[0] = (mm(t0[1], r0[...]) - mm(t0[0], x1)).astype(BF)

    @pl.when(z % 2 == 0)
    def _():
        out[1] = x1

    @pl.when(z == 1)
    def _():
        out[1] = x2

    @pl.when(z == 3)
    def _():
        out[1] = jnp.where(x_hi == 0, x3, x4)


PIECE = 2


def backward_kernel(parts, r, mats, own, got, *refs):
    bases, mts = refs[:parts], refs[parts : 2 * parts]
    leaf_out, root_out, sep_out, small, held, sems, small_sems = refs[2 * parts :]
    core = leaf_place()[0]
    left = jnp.where(core == 0, own[...], got[...])
    right = jnp.where(core == 0, got[...], own[...])
    parent = jnp.concatenate([left[0], right[0]], axis=1)
    small[0] = (mm(mats[1], r[...]) - mmt(mats[0], parent)).astype(BF)
    small[1] = jnp.where(core == 0, parent, jnp.concatenate([left[1], right[1]], axis=1))
    copies = [
        pltpu.make_async_copy(small.at[n], ref.at[0], small_sems.at[n])
        for n, ref in enumerate((root_out, sep_out))
    ]
    for copy in copies:
        copy.start()
    count = 24 // PIECE
    for step in range(count):
        part, at = divmod(step, count // parts)
        here = pl.ds(at * PIECE, PIECE)
        moved = mm(mts[part][here].reshape(PIECE * 256, 256), small[0])
        held[step] = (bases[part][here].astype(F32) + moved.reshape(PIECE, 256, 512)).astype(BF)
        copy = pltpu.make_async_copy(
            held.at[step], leaf_out.at[pl.ds(step * PIECE, PIECE)], sems.at[step]
        )
        copy.start()
        copies.append(copy)
    for copy in copies:
        copy.wait()


def backward(r, mats, own, got, bases, mts):
    return call(
        functools.partial(backward_kernel, len(bases)),
        [(24, 256, 512), (1, 256, 512), (1, 256, 512)],
        r,
        mats,
        own,
        got,
        *bases,
        *mts,
        scratch=[
            pltpu.VMEM((2, 256, 512), BF),
            pltpu.VMEM((24 // PIECE, PIECE, 256, 512), BF),
            pltpu.SemaphoreType.DMA((24 // PIECE,)),
            pltpu.SemaphoreType.DMA((2,)),
        ],
        out_specs=[ANY] * 3,
        flops=2**31,
        size=2**24,
        limit=14,
    )


def local(
    rhs_leaves,
    rhs_roots,
    rhs_seps,
    above_solution,
    leaf_inverse,
    leaf_update,
    leaf_rows,
    root_inverse,
    root_coupling,
    sep_inverse,
    sep_coupling,
):
    w, small = call(
        pack_kernel,
        [(24, 48, 256), (8, 128, 256)],
        root_inverse,
        root_coupling,
        sep_inverse,
        sep_coupling,
        leaf_inverse,
        leaf_update,
        scratch=[pltpu.SemaphoreType.DMA((34,))],
        limit=56,
        in_specs=[ANY] * 6,
    )
    small = lax.all_to_all(small, "load", 0, 0)
    arrived = up(w), down(w), across(w), small
    staged = w, leaf_rows.reshape(24, 1, 128), rhs_seps
    staged = call(
        stage_kernel,
        [shape(v.shape, v.dtype) for v in staged],
        *staged,
        scratch=[pltpu.SemaphoreType.DMA((len(staged),))],
        in_specs=[ANY] * len(staged),
    )
    arrived, staged = lax.optimization_barrier((arrived, staged))
    a, b, c, small = arrived
    w, lists, rhs_seps = staged
    d, e, f = lax.optimization_barrier((up(a), across(a), down(c)))
    g, h = up(e[:HALF]), down(f[HALF:])
    blocks = (w, a, b, c, d, e, f)
    root_mats, keep, send = call(
        small_kernel, [(2, 256, 256), (3, 256, 256), (3, 256, 256)], small, rhs_seps, rhs_leaves
    )

    over_z = lambda v: [among(v, z_shift(k)) for k in (1, 2, 3)]
    even, odd, part = call(
        sides_kernel,
        [(3, 256, 256), (3, 256, 256), (2, 256, 256)],
        keep,
        among(send, CORES),
    )
    packs = over_z(part)
    m, inv, total = leaves_forward(
        (*blocks, g, h), rhs_leaves, lists
    )

    r_root, flow, send = call(
        root_kernel, [(256, 512), (256, 256), (256, 256)], rhs_roots, total, root_mats
    )
    packs2 = [among(v, CORES) for v in packs]
    theirs, packs, packs2 = lax.optimization_barrier((among(send, CORES), packs, packs2))
    top, carried = call(
        choose_kernel, [(3, 256, 256), (2, 256, 256)], odd, part, *packs, *packs2
    )
    far = among(carried, X_HI)
    r0, flow, t0 = call(
        first_kernel,
        [(256, 256), (256, 256), (2, 256, 256)],
        even,
        flow,
        theirs,
    )
    flows = over_z(flow)
    held, flow = lax.optimization_barrier((inv, flow))
    parts = [prepare(8 * n, 8, held, m, rhs_leaves) for n in range(2)]
    flows, parts = lax.optimization_barrier((flows, parts))
    r, flow, t = call(
        middle_kernel,
        [(2, 256, 256), (256, 256), (2, 2, 256, 256)],
        odd,
        *packs,
        *packs2,
        flow,
        *flows,
    )
    far, flow = lax.optimization_barrier((far, flow))
    theirs = among(flow, X_HI)
    far2 = among(far, CORES)
    held, flow = lax.optimization_barrier((held, flow))
    parts.append(prepare(16, 8, held, m, rhs_leaves))
    theirs, parts = lax.optimization_barrier((theirs, parts))
    (own,) = call(
        top_kernel,
        [(2, 256, 256)],
        flow,
        theirs,
        top,
        far,
        far2,
        t0,
        t,
        r0,
        r,
        above_solution,
        scratch=[pltpu.VMEM((3, 256, 256), BF)] * 2,
    )
    return tuple(
        backward(
            r_root,
            root_mats,
            own,
            among(own, CORES),
            [p[0] for p in parts],
            [p[1] for p in parts],
        )
    )


def solution(mesh):
    rows = P("leaf", "load", None)
    columns = P("leaf", None, "load")
    in_specs = (columns, columns, columns, P(None, "load"), rows, rows, P("leaf", None)) + (rows,) * 4
    return jax.shard_map(
        local, mesh=mesh, in_specs=in_specs, out_specs=(columns,) * 3, check_vma=False
    )
```

```python
import functools

import jax
import jax.numpy as jnp
from jax import lax
from jax.experimental import pallas as pl
from jax.experimental.pallas import tpu as pltpu
from jax.sharding import PartitionSpec as P

BF = jnp.bfloat16
F32 = jnp.float32


def mm(a, b):
    return jnp.dot(a, b, preferred_element_type=F32)


def mmt(a, b):
    return lax.dot_general(a, b, (((0,), (0,)), ((), ())), preferred_element_type=F32)


def sub(rhs, inflow):
    return (rhs.astype(F32) - inflow).astype(BF)


def f32sum(a, b):
    return a.astype(F32) + b.astype(F32)


def y_shift(s):
    return [(x * 4 + y, x * 4 + (y + s) % 4) for x in range(2) for y in range(4)]


def z_shift(s):
    return [
        (x * 8 + z * 2 + c, x * 8 + (z + s) % 4 * 2 + c)
        for x in range(2)
        for z in range(4)
        for c in range(2)
    ]


X_LO = [(p, (p + 4) % 8) for p in range(8)]
X_HI = [(p, (p + 8) % 16) for p in range(16)]
CORES = [(p, p ^ 1) for p in range(16)]


def up(v):
    return lax.ppermute(v, "load", y_shift(1))


def down(v):
    return lax.ppermute(v, "load", y_shift(3))


def across(v):
    return lax.ppermute(v, "load", X_LO)


def among(v, pairs):
    return lax.ppermute(v, "leaf", pairs)


def shape(dims, dtype=BF):
    return jax.ShapeDtypeStruct(dims, dtype)


VMEM = pl.BlockSpec(memory_space=pltpu.VMEM)
ANY = pl.BlockSpec(memory_space=pl.ANY)


def call(kernel, outs, *args, scratch=(), flops=2**26, limit=8, size=2**20, **specs):
    return pl.pallas_call(
        kernel,
        in_specs=specs.get("in_specs", [VMEM] * len(args)),
        out_specs=specs.get("out_specs", [VMEM] * len(outs)),
        out_shape=[o if isinstance(o, jax.ShapeDtypeStruct) else shape(o) for o in outs],
        scratch_shapes=list(scratch),
        compiler_params=pltpu.CompilerParams(vmem_limit_bytes=limit * 2**20),
        cost_estimate=pl.CostEstimate(flops=flops, bytes_accessed=size, transcendentals=0),
    )(*args)


ORIGINS = [(0, 0), (0, 3), (0, 1), (1, 0), (0, 2), (1, 3), (1, 1), (1, 2)]


def origin(slot):
    load = lax.axis_index("load")
    dx, dy = ORIGINS[slot]
    return lax.rem(load // 4 + dx, 2) * 4 + lax.rem(load + dy, 4)


def leaf_place():
    position = lax.axis_index("leaf")
    return lax.rem(position, 2), lax.rem(position // 2, 4), position // 8


def pack_kernel(inv, upd, out, sems):
    move([(inv, out.at[:, pl.ds(0, 32)]), (upd, out.at[:, pl.ds(32, 16)])], sems)


def pack_small_kernel(*refs):
    smalls, (out, sems) = refs[:4], refs[4:]
    pairs = []
    for n, ref in enumerate(smalls):
        for to in range(8):
            pairs.append((ref.at[0], out.at[to, pl.ds(32 * n, 32)]))
    move(pairs, sems)


def move(pairs, sems):
    copies = [pltpu.make_async_copy(a, b, sems.at[n]) for n, (a, b) in enumerate(pairs)]
    for copy in copies:
        copy.start()
    for copy in copies:
        copy.wait()


def by_core(whole, keep, send):
    core = leaf_place()[0]
    for c in range(2):

        @pl.when(core == c)
        def _():
            keep[...] = whole[:, 256 * c : 256 * c + 256]
            send[...] = whole[:, 256 - 256 * c : 512 - 256 * c]


def small_kernel(rows, rhs, leaves, root_ref, keep, send):
    del leaves
    full = [
        jnp.concatenate([rows[d, 32 * m : 32 * m + 32, :] for d in range(8)], axis=0)
        for m in range(4)
    ]
    for m, outs in ((0, (root_ref,)), (2, (keep, send))):
        inv, cpl = full[m], full[m + 1]
        for n, value in enumerate((mm(cpl, inv).astype(BF), mmt(inv, inv).astype(BF))):
            for out in outs:
                out[n] = value
    by_core(rhs[0], keep.at[2], send.at[2])


def sides_kernel(own, got, even, odd, part):
    core = leaf_place()[0]
    for c, (a, b) in enumerate(((own, got), (got, own))):

        @pl.when(core == c)
        def _():
            even[...] = a[...]
            odd[...] = b[...]
            part[0] = b[c]
            part[1] = b[2]


def joined(core, mine, theirs):
    a = jnp.where(core == 0, mine[0], theirs[0])
    g = jnp.where(core == 0, theirs[0], mine[0])
    return a, g, mine[1]


def stage_kernel(*refs):
    n = len(refs) // 2
    ins, outs, sems = refs[:n], refs[n:-1], refs[-1]
    copies = [pltpu.make_async_copy(a, b, sems.at[n]) for n, (a, b) in enumerate(zip(ins, outs))]
    for copy in copies:
        copy.start()
    for copy in copies:
        copy.wait()


HALF = 12


def forward_kernel(*refs):
    common, last = refs[:7], refs[7:9]
    rhs, rows, m_ref, inv, total, upd = refs[9:]
    for n in range(2):
        first = n * HALF
        for slot in range(8):
            if slot < 7:
                rows48 = common[slot][pl.ds(first, HALF)]
            else:
                rows48 = last[n][...]
            at = origin(slot)
            inv[pl.ds(first, HALF), pl.ds(pl.multiple_of(at * 32, 32), 32), :] = rows48[:, :32]
            upd[:, pl.ds(pl.multiple_of(at * 16, 16), 16), :] = rows48[:, 32:]
        flows = [mm(upd[i], inv[first + i]).astype(BF) for i in range(HALF)]
        parts = []
        for i in range(HALF):
            hot = lax.broadcasted_iota(jnp.int32, (256, 128), 0) == rows[first + i]
            m = mm(hot.astype(BF), flows[i]).astype(BF)
            m_ref[first + i] = m
            parts.append(m)
        new = mm(
            jnp.concatenate(parts, axis=1), rhs[pl.ds(first, HALF)].reshape(HALF * 256, 512)
        )
        total[...] = new if n == 0 else total[...] + new


def leaves_forward(blocks, rhs, rows):
    return call(
        forward_kernel,
        [(24, 256, 256), (24, 256, 256), shape((256, 512), F32)],
        *blocks,
        rhs,
        rows,
        scratch=[
            pltpu.VMEM((HALF, 128, 256), BF),
        ],
        flops=2**20,
        size=2**24,
        limit=16,
    )


def prepare_kernel(first, inv, m, rhs, base, mt):
    count = base.shape[0]
    squares = [mmt(inv[first + i], inv[first + i]).astype(BF) for i in range(count)]
    for i in range(count):
        mt[i] = -(m[first + i].T)
    for i in range(count):
        base[i] = mm(squares[i], rhs[first + i]).astype(BF)


def prepare(first, count, inv, m, rhs):
    return call(
        functools.partial(prepare_kernel, first),
        [(count, 256, 512), (count, 256, 256)],
        inv,
        m,
        rhs,
        flops=count * 2**27,
    )


def root_kernel(rhs, total, mats, r_ref, keep, send):
    r = sub(rhs[0], total[...])
    r_ref[...] = r
    by_core(mm(mats[0], r).astype(BF), keep, send)


def first_kernel(pack, mine, theirs, r_ref, flow, mats):
    r = sub(pack[2], f32sum(mine[...], theirs[...]))
    r_ref[...] = r
    flow[...] = mm(pack[0], r).astype(BF)
    mats[0] = pack[0].T
    mats[1] = pack[1]


def middle_kernel(odd, *refs):
    mine, theirs, flows, (r_ref, flow, mats) = refs[:3], refs[3:6], refs[6:10], refs[10:]
    core, z, _ = leaf_place()
    for k in range(4):

        @pl.when(z == k)
        def _():
            p = []
            for j in range(4):
                n = (k - j) % 4
                p.append(joined(core, mine[n - 1], theirs[n - 1]) if n else odd)
            f = [flows[(k - j) % 4] for j in range(4)]
            r = [None] * 3
            out = [None] * 3
            for j in (0, 2):
                r[j] = sub(p[j][2], f32sum(f[j][...], f[j + 1][...]))
                out[j] = mm(p[j][0], r[j]).astype(BF)
            r[1] = sub(p[1][2], f32sum(out[0], out[2]))
            flow[...] = mm(p[1][0], r[1]).astype(BF)
            for n, j in enumerate((k // 2 * 2, 1)):
                r_ref[n] = r[j]
                mats[n, 0] = p[j][0].T
                mats[n, 1] = p[j][1]


def choose_kernel(odd, *refs):
    mine, theirs, top = refs[:3], refs[3:6], refs[6]
    core, z, _ = leaf_place()

    @pl.when(z == 3)
    def _():
        top[...] = odd[...]

    for k in range(3):

        @pl.when(z == k)
        def _():
            for n, value in enumerate(joined(core, mine[k], theirs[k])):
                top[n] = value


def top_kernel(mine, theirs, top, far, t0, t, r0, r, above, out, p3, p4):
    core, z, x_hi = leaf_place()
    above = above[:, pl.ds(pl.multiple_of(core * 256, 256), 256)]
    for h, (a, b) in enumerate(((p3, p4), (p4, p3))):

        @pl.when(x_hi == h)
        def _():
            a[...] = top[...]
            b[...] = far[...]

    r3 = sub(p3[2], f32sum(mine[...], theirs[...]))
    r4 = sub(p4[2], mm(p3[0], r3).astype(BF).astype(F32))
    x4 = (mm(p4[1], r4) - mmt(p4[0], above)).astype(BF)
    x3 = (mm(p3[1], r3) - mmt(p3[0], x4)).astype(BF)
    x2 = (mm(t[1, 1], r[1]) - mm(t[1, 0], x3)).astype(BF)
    x1 = (mm(t[0, 1], r[0]) - mm(t[0, 0], x2)).astype(BF)
    out[0] = (mm(t0[1], r0[...]) - mm(t0[0], x1)).astype(BF)

    @pl.when(z % 2 == 0)
    def _():
        out[1] = x1

    @pl.when(z == 1)
    def _():
        out[1] = x2

    @pl.when(z == 3)
    def _():
        out[1] = jnp.where(x_hi == 0, x3, x4)


PIECE = 2


def backward_kernel(parts, r, mats, own, got, *refs):
    bases, mts = refs[:parts], refs[parts : 2 * parts]
    leaf_out, root_out, sep_out, small, held, sems, small_sems = refs[2 * parts :]
    core = leaf_place()[0]
    left = jnp.where(core == 0, own[...], got[...])
    right = jnp.where(core == 0, got[...], own[...])
    parent = jnp.concatenate([left[0], right[0]], axis=1)
    small[0] = (mm(mats[1], r[...]) - mmt(mats[0], parent)).astype(BF)
    small[1] = jnp.where(core == 0, parent, jnp.concatenate([left[1], right[1]], axis=1))
    copies = [
        pltpu.make_async_copy(small.at[n], ref.at[0], small_sems.at[n])
        for n, ref in enumerate((root_out, sep_out))
    ]
    for copy in copies:
        copy.start()
    count = 24 // PIECE
    for step in range(count):
        part, at = divmod(step, count // parts)
        here = pl.ds(at * PIECE, PIECE)
        moved = mm(mts[part][here].reshape(PIECE * 256, 256), small[0])
        held[step] = (bases[part][here].astype(F32) + moved.reshape(PIECE, 256, 512)).astype(BF)
        copy = pltpu.make_async_copy(
            held.at[step], leaf_out.at[pl.ds(step * PIECE, PIECE)], sems.at[step]
        )
        copy.start()
        copies.append(copy)
    for copy in copies:
        copy.wait()


def backward(r, mats, own, got, bases, mts):
    return call(
        functools.partial(backward_kernel, len(bases)),
        [(24, 256, 512), (1, 256, 512), (1, 256, 512)],
        r,
        mats,
        own,
        got,
        *bases,
        *mts,
        scratch=[
            pltpu.VMEM((2, 256, 512), BF),
            pltpu.VMEM((24 // PIECE, PIECE, 256, 512), BF),
            pltpu.SemaphoreType.DMA((24 // PIECE,)),
            pltpu.SemaphoreType.DMA((2,)),
        ],
        out_specs=[ANY] * 3,
        flops=2**31,
        size=2**24,
        limit=14,
    )


def local(
    rhs_leaves,
    rhs_roots,
    rhs_seps,
    above_solution,
    leaf_inverse,
    leaf_update,
    leaf_rows,
    root_inverse,
    root_coupling,
    sep_inverse,
    sep_coupling,
):
    (w,) = call(
        pack_kernel,
        [(24, 48, 256)],
        leaf_inverse,
        leaf_update,
        scratch=[pltpu.SemaphoreType.DMA((2,))],
        limit=56,
        in_specs=[ANY] * 2,
    )
    (small,) = call(
        pack_small_kernel,
        [(8, 128, 256)],
        root_inverse,
        root_coupling,
        sep_inverse,
        sep_coupling,
        scratch=[pltpu.SemaphoreType.DMA((32,))],
        limit=56,
        in_specs=[ANY] * 4,
    )
    small = lax.all_to_all(small, "load", 0, 0)
    arrived = up(w), down(w), across(w), small
    staged = w, leaf_rows.reshape(24, 1, 128), rhs_seps
    staged = call(
        stage_kernel,
        [shape(v.shape, v.dtype) for v in staged],
        *staged,
        scratch=[pltpu.SemaphoreType.DMA((len(staged),))],
        in_specs=[ANY] * len(staged),
    )
    arrived, staged = lax.optimization_barrier((arrived, staged))
    a, b, c, small = arrived
    w, lists, rhs_seps = staged
    d, e, f = lax.optimization_barrier((up(a), across(a), down(c)))
    g, h = up(e[:HALF]), down(f[HALF:])
    blocks = (w, a, b, c, d, e, f)
    root_mats, keep, send = call(
        small_kernel, [(2, 256, 256), (3, 256, 256), (3, 256, 256)], small, rhs_seps, rhs_leaves
    )

    over_z = lambda v: [among(v, z_shift(k)) for k in (1, 2, 3)]
    even, odd, part = call(
        sides_kernel,
        [(3, 256, 256), (3, 256, 256), (2, 256, 256)],
        keep,
        among(send, CORES),
    )
    packs = over_z(part)
    m, inv, total = leaves_forward(
        (*blocks, g, h), rhs_leaves, lists
    )

    r_root, flow, send = call(
        root_kernel, [(256, 512), (256, 256), (256, 256)], rhs_roots, total, root_mats
    )
    packs2 = [among(v, CORES) for v in packs]
    theirs, packs, packs2 = lax.optimization_barrier((among(send, CORES), packs, packs2))
    (top,) = call(
        choose_kernel, [(3, 256, 256)], odd, *packs, *packs2
    )
    far = among(top, X_HI)
    r0, flow, t0 = call(
        first_kernel,
        [(256, 256), (256, 256), (2, 256, 256)],
        even,
        flow,
        theirs,
    )
    flows = over_z(flow)
    held, flow = lax.optimization_barrier((inv, flow))
    parts = [prepare(8 * n, 8, held, m, rhs_leaves) for n in range(2)]
    flows, parts = lax.optimization_barrier((flows, parts))
    r, flow, t = call(
        middle_kernel,
        [(2, 256, 256), (256, 256), (2, 2, 256, 256)],
        odd,
        *packs,
        *packs2,
        flow,
        *flows,
    )
    theirs = among(flow, X_HI)
    held, flow = lax.optimization_barrier((held, flow))
    parts.append(prepare(16, 8, held, m, rhs_leaves))
    theirs, parts = lax.optimization_barrier((theirs, parts))
    (own,) = call(
        top_kernel,
        [(2, 256, 256)],
        flow,
        theirs,
        top,
        far,
        t0,
        t,
        r0,
        r,
        above_solution,
        scratch=[pltpu.VMEM((3, 256, 256), BF)] * 2,
    )
    return tuple(
        backward(
            r_root,
            root_mats,
            own,
            among(own, CORES),
            [p[0] for p in parts],
            [p[1] for p in parts],
        )
    )


def solution(mesh):
    rows = P("leaf", "load", None)
    columns = P("leaf", None, "load")
    in_specs = (columns, columns, columns, P(None, "load"), rows, rows, P("leaf", None)) + (rows,) * 4
    return jax.shard_map(
        local, mesh=mesh, in_specs=in_specs, out_specs=(columns,) * 3, check_vma=False
    )
```

```python
import functools

import jax
import jax.numpy as jnp
from jax import lax
from jax.experimental import pallas as pl
from jax.experimental.pallas import tpu as pltpu
from jax.sharding import PartitionSpec as P

BF = jnp.bfloat16
F32 = jnp.float32


def mm(a, b):
    return jnp.dot(a, b, preferred_element_type=F32)


def mmt(a, b):
    return lax.dot_general(a, b, (((0,), (0,)), ((), ())), preferred_element_type=F32)


def sub(rhs, inflow):
    return (rhs.astype(F32) - inflow).astype(BF)


def f32sum(a, b):
    return a.astype(F32) + b.astype(F32)


def y_shift(s):
    return [(x * 4 + y, x * 4 + (y + s) % 4) for x in range(2) for y in range(4)]


def z_shift(s):
    return [
        (x * 8 + z * 2 + c, x * 8 + (z + s) % 4 * 2 + c)
        for x in range(2)
        for z in range(4)
        for c in range(2)
    ]


X_LO = [(p, (p + 4) % 8) for p in range(8)]
X_HI = [(p, (p + 8) % 16) for p in range(16)]
CORES = [(p, p ^ 1) for p in range(16)]


def up(v):
    return lax.ppermute(v, "load", y_shift(1))


def down(v):
    return lax.ppermute(v, "load", y_shift(3))


def across(v):
    return lax.ppermute(v, "load", X_LO)


def among(v, pairs):
    return lax.ppermute(v, "leaf", pairs)


def shape(dims, dtype=BF):
    return jax.ShapeDtypeStruct(dims, dtype)


VMEM = pl.BlockSpec(memory_space=pltpu.VMEM)
ANY = pl.BlockSpec(memory_space=pl.ANY)


def call(kernel, outs, *args, scratch=(), flops=2**26, limit=8, size=2**20, **specs):
    return pl.pallas_call(
        kernel,
        in_specs=specs.get("in_specs", [VMEM] * len(args)),
        out_specs=specs.get("out_specs", [VMEM] * len(outs)),
        out_shape=[o if isinstance(o, jax.ShapeDtypeStruct) else shape(o) for o in outs],
        scratch_shapes=list(scratch),
        compiler_params=pltpu.CompilerParams(vmem_limit_bytes=limit * 2**20),
        cost_estimate=pl.CostEstimate(flops=flops, bytes_accessed=size, transcendentals=0),
    )(*args)


ORIGINS = [(0, 0), (0, 3), (0, 1), (1, 0), (0, 2), (1, 3), (1, 1), (1, 2)]


def origin(slot):
    load = lax.axis_index("load")
    dx, dy = ORIGINS[slot]
    return lax.rem(load // 4 + dx, 2) * 4 + lax.rem(load + dy, 4)


def leaf_place():
    position = lax.axis_index("leaf")
    return lax.rem(position, 2), lax.rem(position // 2, 4), position // 8


def pack_kernel(inv, upd, out, sems):
    move([(inv, out.at[:, pl.ds(0, 32)]), (upd, out.at[:, pl.ds(32, 16)])], sems)


def pack_small_kernel(*refs):
    smalls, (out, held, sems) = refs[:4], refs[4:]
    move([(ref.at[0], held.at[pl.ds(32 * n, 32)]) for n, ref in enumerate(smalls)], sems)
    move([(held, out.at[n]) for n in range(8)], sems)


def move(pairs, sems):
    copies = [pltpu.make_async_copy(a, b, sems.at[n]) for n, (a, b) in enumerate(pairs)]
    for copy in copies:
        copy.start()
    for copy in copies:
        copy.wait()


def by_core(whole, keep, send):
    core = leaf_place()[0]
    for c in range(2):

        @pl.when(core == c)
        def _():
            keep[...] = whole[:, 256 * c : 256 * c + 256]
            send[...] = whole[:, 256 - 256 * c : 512 - 256 * c]


def small_kernel(rows, rhs, leaves, root_ref, keep, send):
    del leaves
    full = [
        jnp.concatenate([rows[d, 32 * m : 32 * m + 32, :] for d in range(8)], axis=0)
        for m in range(4)
    ]
    for m, outs in ((0, (root_ref,)), (2, (keep, send))):
        inv, cpl = full[m], full[m + 1]
        for n, value in enumerate((mm(cpl, inv).astype(BF), mmt(inv, inv).astype(BF))):
            for out in outs:
                out[n] = value
    by_core(rhs[0], keep.at[2], send.at[2])


def sides_kernel(own, got, even, odd, part):
    core = leaf_place()[0]
    for c, (a, b) in enumerate(((own, got), (got, own))):

        @pl.when(core == c)
        def _():
            even[...] = a[...]
            odd[...] = b[...]
            part[0] = b[c]
            part[1] = b[2]


def joined(core, mine, theirs):
    a = jnp.where(core == 0, mine[0], theirs[0])
    g = jnp.where(core == 0, theirs[0], mine[0])
    return a, g, mine[1]


def stage_kernel(*refs):
    n = len(refs) // 2
    ins, outs, sems = refs[:n], refs[n:-1], refs[-1]
    copies = [pltpu.make_async_copy(a, b, sems.at[n]) for n, (a, b) in enumerate(zip(ins, outs))]
    for copy in copies:
        copy.start()
    for copy in copies:
        copy.wait()


HALF = 12


def forward_kernel(*refs):
    common, last = refs[:7], refs[7:9]
    rhs, rows, m_ref, inv, total, upd = refs[9:]
    for n in range(2):
        first = n * HALF
        for slot in range(8):
            if slot < 7:
                rows48 = common[slot][pl.ds(first, HALF)]
            else:
                rows48 = last[n][...]
            at = origin(slot)
            inv[pl.ds(first, HALF), pl.ds(pl.multiple_of(at * 32, 32), 32), :] = rows48[:, :32]
            upd[:, pl.ds(pl.multiple_of(at * 16, 16), 16), :] = rows48[:, 32:]
        flows = [mm(upd[i], inv[first + i]).astype(BF) for i in range(HALF)]
        parts = []
        for i in range(HALF):
            hot = lax.broadcasted_iota(jnp.int32, (256, 128), 0) == rows[first + i]
            m = mm(hot.astype(BF), flows[i]).astype(BF)
            m_ref[first + i] = m
            parts.append(m)
        new = mm(
            jnp.concatenate(parts, axis=1), rhs[pl.ds(first, HALF)].reshape(HALF * 256, 512)
        )
        total[...] = new if n == 0 else total[...] + new


def leaves_forward(blocks, rhs, rows):
    return call(
        forward_kernel,
        [(24, 256, 256), (24, 256, 256), shape((256, 512), F32)],
        *blocks,
        rhs,
        rows,
        scratch=[
            pltpu.VMEM((HALF, 128, 256), BF),
        ],
        flops=2**20,
        size=2**24,
        limit=16,
    )


def prepare_kernel(first, inv, m, rhs, base, mt):
    count = base.shape[0]
    squares = [mmt(inv[first + i], inv[first + i]).astype(BF) for i in range(count)]
    for i in range(count):
        mt[i] = -(m[first + i].T)
    for i in range(count):
        base[i] = mm(squares[i], rhs[first + i]).astype(BF)


def prepare(first, count, inv, m, rhs):
    return call(
        functools.partial(prepare_kernel, first),
        [(count, 256, 512), (count, 256, 256)],
        inv,
        m,
        rhs,
        flops=count * 2**27,
    )


def root_kernel(rhs, total, mats, r_ref, keep, send):
    r = sub(rhs[0], total[...])
    r_ref[...] = r
    by_core(mm(mats[0], r).astype(BF), keep, send)


def first_kernel(pack, mine, theirs, r_ref, flow, mats):
    r = sub(pack[2], f32sum(mine[...], theirs[...]))
    r_ref[...] = r
    flow[...] = mm(pack[0], r).astype(BF)
    mats[0] = pack[0].T
    mats[1] = pack[1]


def middle_kernel(odd, *refs):
    mine, theirs, flows, (r_ref, flow, mats) = refs[:3], refs[3:6], refs[6:10], refs[10:]
    core, z, _ = leaf_place()
    for k in range(4):

        @pl.when(z == k)
        def _():
            p = []
            for j in range(4):
                n = (k - j) % 4
                p.append(joined(core, mine[n - 1], theirs[n - 1]) if n else odd)
            f = [flows[(k - j) % 4] for j in range(4)]
            r = [None] * 3
            out = [None] * 3
            for j in (0, 2):
                r[j] = sub(p[j][2], f32sum(f[j][...], f[j + 1][...]))
                out[j] = mm(p[j][0], r[j]).astype(BF)
            r[1] = sub(p[1][2], f32sum(out[0], out[2]))
            flow[...] = mm(p[1][0], r[1]).astype(BF)
            for n, j in enumerate((k // 2 * 2, 1)):
                r_ref[n] = r[j]
                mats[n, 0] = p[j][0].T
                mats[n, 1] = p[j][1]


def choose_kernel(odd, *refs):
    mine, theirs, top = refs[:3], refs[3:6], refs[6]
    core, z, _ = leaf_place()

    @pl.when(z == 3)
    def _():
        top[...] = odd[...]

    for k in range(3):

        @pl.when(z == k)
        def _():
            for n, value in enumerate(joined(core, mine[k], theirs[k])):
                top[n] = value


def top_kernel(mine, theirs, top, far, t0, t, r0, r, above, out):
    core, z, x_hi = leaf_place()
    above = above[:, pl.ds(pl.multiple_of(core * 256, 256), 256)]
    for h, (p3, p4) in enumerate(((top, far), (far, top))):

        @pl.when(x_hi == h)
        def _():
            r3 = sub(p3[2], f32sum(mine[...], theirs[...]))
            r4 = sub(p4[2], mm(p3[0], r3).astype(BF).astype(F32))
            x4 = (mm(p4[1], r4) - mmt(p4[0], above)).astype(BF)
            x3 = (mm(p3[1], r3) - mmt(p3[0], x4)).astype(BF)
            x2 = (mm(t[1, 1], r[1]) - mm(t[1, 0], x3)).astype(BF)
            x1 = (mm(t[0, 1], r[0]) - mm(t[0, 0], x2)).astype(BF)
            out[0] = (mm(t0[1], r0[...]) - mm(t0[0], x1)).astype(BF)
            out[1] = jnp.where(z % 2 == 0, x1, jnp.where(z == 1, x2, x4 if h else x3))


PIECE = 2


def backward_kernel(parts, r, mats, own, got, *refs):
    bases, mts = refs[:parts], refs[parts : 2 * parts]
    leaf_out, root_out, sep_out, small, held, sems, small_sems = refs[2 * parts :]
    core = leaf_place()[0]
    left = jnp.where(core == 0, own[...], got[...])
    right = jnp.where(core == 0, got[...], own[...])
    parent = jnp.concatenate([left[0], right[0]], axis=1)
    small[0] = (mm(mats[1], r[...]) - mmt(mats[0], parent)).astype(BF)
    small[1] = jnp.where(core == 0, parent, jnp.concatenate([left[1], right[1]], axis=1))
    copies = [
        pltpu.make_async_copy(small.at[n], ref.at[0], small_sems.at[n])
        for n, ref in enumerate((root_out, sep_out))
    ]
    for copy in copies:
        copy.start()
    count = 24 // PIECE
    for step in range(count):
        part, at = divmod(step, count // parts)
        here = pl.ds(at * PIECE, PIECE)
        moved = mm(mts[part][here].reshape(PIECE * 256, 256), small[0])
        held[step] = (bases[part][here].astype(F32) + moved.reshape(PIECE, 256, 512)).astype(BF)
        copy = pltpu.make_async_copy(
            held.at[step], leaf_out.at[pl.ds(step * PIECE, PIECE)], sems.at[step]
        )
        copy.start()
        copies.append(copy)
    for copy in copies:
        copy.wait()


def backward(r, mats, own, got, bases, mts):
    return call(
        functools.partial(backward_kernel, len(bases)),
        [(24, 256, 512), (1, 256, 512), (1, 256, 512)],
        r,
        mats,
        own,
        got,
        *bases,
        *mts,
        scratch=[
            pltpu.VMEM((2, 256, 512), BF),
            pltpu.VMEM((24 // PIECE, PIECE, 256, 512), BF),
            pltpu.SemaphoreType.DMA((24 // PIECE,)),
            pltpu.SemaphoreType.DMA((2,)),
        ],
        out_specs=[ANY] * 3,
        flops=2**31,
        size=2**24,
        limit=14,
    )


def local(
    rhs_leaves,
    rhs_roots,
    rhs_seps,
    above_solution,
    leaf_inverse,
    leaf_update,
    leaf_rows,
    root_inverse,
    root_coupling,
    sep_inverse,
    sep_coupling,
):
    (w,) = call(
        pack_kernel,
        [(24, 48, 256)],
        leaf_inverse,
        leaf_update,
        scratch=[pltpu.SemaphoreType.DMA((2,))],
        limit=56,
        in_specs=[ANY] * 2,
    )
    (small,) = call(
        pack_small_kernel,
        [(8, 128, 256)],
        root_inverse,
        root_coupling,
        sep_inverse,
        sep_coupling,
        scratch=[pltpu.VMEM((128, 256), BF), pltpu.SemaphoreType.DMA((8,))],
        limit=56,
        in_specs=[ANY] * 4,
    )
    small = lax.all_to_all(small, "load", 0, 0)
    arrived = up(w), down(w), across(w), small
    staged = w, leaf_rows.reshape(24, 1, 128), rhs_seps
    staged = call(
        stage_kernel,
        [shape(v.shape, v.dtype) for v in staged],
        *staged,
        scratch=[pltpu.SemaphoreType.DMA((len(staged),))],
        in_specs=[ANY] * len(staged),
    )
    arrived, staged = lax.optimization_barrier((arrived, staged))
    a, b, c, small = arrived
    w, lists, rhs_seps = staged
    d, e, f = lax.optimization_barrier((up(a), across(a), down(c)))
    g, h = up(e[:HALF]), down(f[HALF:])
    blocks = (w, a, b, c, d, e, f)
    root_mats, keep, send = call(
        small_kernel, [(2, 256, 256), (3, 256, 256), (3, 256, 256)], small, rhs_seps, rhs_leaves
    )

    over_z = lambda v: [among(v, z_shift(k)) for k in (1, 2, 3)]
    even, odd, part = call(
        sides_kernel,
        [(3, 256, 256), (3, 256, 256), (2, 256, 256)],
        keep,
        among(send, CORES),
    )
    packs = over_z(part)
    m, inv, total = leaves_forward(
        (*blocks, g, h), rhs_leaves, lists
    )

    r_root, flow, send = call(
        root_kernel, [(256, 512), (256, 256), (256, 256)], rhs_roots, total, root_mats
    )
    packs2 = [among(v, CORES) for v in packs]
    theirs, even, odd = lax.optimization_barrier((among(send, CORES), even, odd))
    (top,) = call(
        choose_kernel, [(3, 256, 256)], odd, *packs, *packs2
    )
    far = among(top, X_HI)
    r0, flow, t0 = call(
        first_kernel,
        [(256, 256), (256, 256), (2, 256, 256)],
        even,
        flow,
        theirs,
    )
    flows = over_z(flow)
    held, flow = lax.optimization_barrier((inv, flow))
    parts = [prepare(8 * n, 8, held, m, rhs_leaves) for n in range(2)]
    flows, parts = lax.optimization_barrier((flows, parts))
    r, flow, t = call(
        middle_kernel,
        [(2, 256, 256), (256, 256), (2, 2, 256, 256)],
        odd,
        *packs,
        *packs2,
        flow,
        *flows,
    )
    theirs = among(flow, X_HI)
    held, flow = lax.optimization_barrier((held, flow))
    parts.append(prepare(16, 8, held, m, rhs_leaves))
    theirs, parts = lax.optimization_barrier((theirs, parts))
    (own,) = call(
        top_kernel,
        [(2, 256, 256)],
        flow,
        theirs,
        top,
        far,
        t0,
        t,
        r0,
        r,
        above_solution,
    )
    return tuple(
        backward(
            r_root,
            root_mats,
            own,
            among(own, CORES),
            [p[0] for p in parts],
            [p[1] for p in parts],
        )
    )


def solution(mesh):
    rows = P("leaf", "load", None)
    columns = P("leaf", None, "load")
    in_specs = (columns, columns, columns, P(None, "load"), rows, rows, P("leaf", None)) + (rows,) * 4
    return jax.shard_map(
        local, mesh=mesh, in_specs=in_specs, out_specs=(columns,) * 3, check_vma=False
    )
```

```python
import functools

import jax
import jax.numpy as jnp
from jax import lax
from jax.experimental import pallas as pl
from jax.experimental.pallas import tpu as pltpu
from jax.sharding import PartitionSpec as P

BF = jnp.bfloat16
F32 = jnp.float32


def mm(a, b):
    return jnp.dot(a, b, preferred_element_type=F32)


def mmt(a, b):
    return lax.dot_general(a, b, (((0,), (0,)), ((), ())), preferred_element_type=F32)


def sub(rhs, inflow):
    return (rhs.astype(F32) - inflow).astype(BF)


def f32sum(a, b):
    return a.astype(F32) + b.astype(F32)


def y_shift(s):
    return [(x * 4 + y, x * 4 + (y + s) % 4) for x in range(2) for y in range(4)]


def z_shift(s):
    return [
        (x * 8 + z * 2 + c, x * 8 + (z + s) % 4 * 2 + c)
        for x in range(2)
        for z in range(4)
        for c in range(2)
    ]


X_LO = [(p, (p + 4) % 8) for p in range(8)]
X_HI = [(p, (p + 8) % 16) for p in range(16)]
CORES = [(p, p ^ 1) for p in range(16)]


def up(v):
    return lax.ppermute(v, "load", y_shift(1))


def down(v):
    return lax.ppermute(v, "load", y_shift(3))


def across(v):
    return lax.ppermute(v, "load", X_LO)


def among(v, pairs):
    return lax.ppermute(v, "leaf", pairs)


def shape(dims, dtype=BF):
    return jax.ShapeDtypeStruct(dims, dtype)


VMEM = pl.BlockSpec(memory_space=pltpu.VMEM)
ANY = pl.BlockSpec(memory_space=pl.ANY)


def call(kernel, outs, *args, scratch=(), flops=2**26, limit=8, size=2**20, **specs):
    return pl.pallas_call(
        kernel,
        in_specs=specs.get("in_specs", [VMEM] * len(args)),
        out_specs=specs.get("out_specs", [VMEM] * len(outs)),
        out_shape=[o if isinstance(o, jax.ShapeDtypeStruct) else shape(o) for o in outs],
        scratch_shapes=list(scratch),
        compiler_params=pltpu.CompilerParams(vmem_limit_bytes=limit * 2**20),
        cost_estimate=pl.CostEstimate(flops=flops, bytes_accessed=size, transcendentals=0),
    )(*args)


ORIGINS = [(0, 0), (0, 3), (0, 1), (1, 0), (0, 2), (1, 3), (1, 1), (1, 2)]


def origin(slot):
    load = lax.axis_index("load")
    dx, dy = ORIGINS[slot]
    return lax.rem(load // 4 + dx, 2) * 4 + lax.rem(load + dy, 4)


def leaf_place():
    position = lax.axis_index("leaf")
    return lax.rem(position, 2), lax.rem(position // 2, 4), position // 8


def pack_kernel(inv, upd, out, sems):
    move([(inv, out.at[:, pl.ds(0, 32)]), (upd, out.at[:, pl.ds(32, 16)])], sems)


def pack_small_kernel(*refs):
    smalls, (out, sems) = refs[:4], refs[4:]
    pairs = []
    for n, ref in enumerate(smalls):
        for to in range(8):
            pairs.append((ref.at[0], out.at[to, pl.ds(32 * n, 32)]))
    move(pairs, sems)


def move(pairs, sems):
    copies = [pltpu.make_async_copy(a, b, sems.at[n]) for n, (a, b) in enumerate(pairs)]
    for copy in copies:
        copy.start()
    for copy in copies:
        copy.wait()


def by_core(whole, keep, send):
    core = leaf_place()[0]
    for c in range(2):

        @pl.when(core == c)
        def _():
            keep[...] = whole[:, 256 * c : 256 * c + 256]
            send[...] = whole[:, 256 - 256 * c : 512 - 256 * c]


def small_kernel(rows, rhs, leaves, root_ref, keep, send):
    del leaves
    full = [
        jnp.concatenate([rows[d, 32 * m : 32 * m + 32, :] for d in range(8)], axis=0)
        for m in range(4)
    ]
    for m, outs in ((0, (root_ref,)), (2, (keep, send))):
        inv, cpl = full[m], full[m + 1]
        for n, value in enumerate((mm(cpl, inv).astype(BF), mmt(inv, inv).astype(BF))):
            for out in outs:
                out[n] = value
    by_core(rhs[0], keep.at[2], send.at[2])


def sides_kernel(own, got, even, odd, part):
    core = leaf_place()[0]
    for c, (a, b) in enumerate(((own, got), (got, own))):

        @pl.when(core == c)
        def _():
            even[...] = a[...]
            odd[...] = b[...]
            part[0] = b[c]
            part[1] = b[2]


def joined(core, mine, theirs):
    a = jnp.where(core == 0, mine[0], theirs[0])
    g = jnp.where(core == 0, theirs[0], mine[0])
    return a, g, mine[1]


def stage_kernel(*refs):
    n = len(refs) // 2
    ins, outs, sems = refs[:n], refs[n:-1], refs[-1]
    copies = [pltpu.make_async_copy(a, b, sems.at[n]) for n, (a, b) in enumerate(zip(ins, outs))]
    for copy in copies:
        copy.start()
    for copy in copies:
        copy.wait()


HALF = 12


def forward_kernel(*refs):
    common, last = refs[:7], refs[7:9]
    rhs, rows, m_ref, inv, total, upd = refs[9:]
    for n in range(2):
        first = n * HALF
        for slot in range(8):
            if slot < 7:
                rows48 = common[slot][pl.ds(first, HALF)]
            else:
                rows48 = last[n][...]
            at = origin(slot)
            inv[pl.ds(first, HALF), pl.ds(pl.multiple_of(at * 32, 32), 32), :] = rows48[:, :32]
            upd[:, pl.ds(pl.multiple_of(at * 16, 16), 16), :] = rows48[:, 32:]
        flows = [mm(upd[i], inv[first + i]).astype(BF) for i in range(HALF)]
        parts = []
        for i in range(HALF):
            hot = lax.broadcasted_iota(jnp.int32, (256, 128), 0) == rows[first + i]
            m = mm(hot.astype(BF), flows[i]).astype(BF)
            m_ref[first + i] = m
            parts.append(m)
        new = mm(
            jnp.concatenate(parts, axis=1), rhs[pl.ds(first, HALF)].reshape(HALF * 256, 512)
        )
        total[...] = new if n == 0 else total[...] + new


def leaves_forward(blocks, rhs, rows):
    return call(
        forward_kernel,
        [(24, 256, 256), (24, 256, 256), shape((256, 512), F32)],
        *blocks,
        rhs,
        rows,
        scratch=[
            pltpu.VMEM((HALF, 128, 256), BF),
        ],
        flops=2**20,
        size=2**24,
        limit=16,
    )


def prepare_kernel(first, inv, m, rhs, base, mt):
    count = base.shape[0]
    squares = [mmt(inv[first + i], inv[first + i]).astype(BF) for i in range(count)]
    for i in range(count):
        mt[i] = -(m[first + i].T)
    for i in range(count):
        base[i] = mm(squares[i], rhs[first + i]).astype(BF)


def prepare(first, count, inv, m, rhs):
    return call(
        functools.partial(prepare_kernel, first),
        [(count, 256, 512), (count, 256, 256)],
        inv,
        m,
        rhs,
        flops=count * 2**27,
    )


def root_kernel(rhs, total, mats, r_ref, keep, send):
    r = sub(rhs[0], total[...])
    r_ref[...] = r
    by_core(mm(mats[0], r).astype(BF), keep, send)


def first_kernel(pack, mine, theirs, r_ref, flow, mats):
    r = sub(pack[2], f32sum(mine[...], theirs[...]))
    r_ref[...] = r
    flow[...] = mm(pack[0], r).astype(BF)
    mats[0] = pack[0].T
    mats[1] = pack[1]


def middle_kernel(odd, *refs):
    mine, theirs, flows, (r_ref, flow, mats) = refs[:3], refs[3:6], refs[6:10], refs[10:]
    core, z, _ = leaf_place()
    for k in range(4):

        @pl.when(z == k)
        def _():
            p = []
            for j in range(4):
                n = (k - j) % 4
                p.append(joined(core, mine[n - 1], theirs[n - 1]) if n else odd)
            f = [flows[(k - j) % 4] for j in range(4)]
            r = [None] * 3
            out = [None] * 3
            for j in (0, 2):
                r[j] = sub(p[j][2], f32sum(f[j][...], f[j + 1][...]))
                out[j] = mm(p[j][0], r[j]).astype(BF)
            r[1] = sub(p[1][2], f32sum(out[0], out[2]))
            flow[...] = mm(p[1][0], r[1]).astype(BF)
            for n, j in enumerate((k // 2 * 2, 1)):
                r_ref[n] = r[j]
                mats[n, 0] = p[j][0].T
                mats[n, 1] = p[j][1]


def choose_kernel(odd, *refs):
    mine, theirs, top = refs[:3], refs[3:6], refs[6]
    core, z, _ = leaf_place()

    @pl.when(z == 3)
    def _():
        top[...] = odd[...]

    for k in range(3):

        @pl.when(z == k)
        def _():
            for n, value in enumerate(joined(core, mine[k], theirs[k])):
                top[n] = value


def top_kernel(mine, theirs, top, far, t0, t, r0, r, above, out, p3, p4):
    core, z, x_hi = leaf_place()
    above = above[:, pl.ds(pl.multiple_of(core * 256, 256), 256)]
    for h, (a, b) in enumerate(((p3, p4), (p4, p3))):

        @pl.when(x_hi == h)
        def _():
            a[...] = top[...]
            b[...] = far[...]

    r3 = sub(p3[2], f32sum(mine[...], theirs[...]))
    r4 = sub(p4[2], mm(p3[0], r3).astype(BF).astype(F32))
    x4 = (mm(p4[1], r4) - mmt(p4[0], above)).astype(BF)
    x3 = (mm(p3[1], r3) - mmt(p3[0], x4)).astype(BF)
    x2 = (mm(t[1, 1], r[1]) - mm(t[1, 0], x3)).astype(BF)
    x1 = (mm(t[0, 1], r[0]) - mm(t[0, 0], x2)).astype(BF)
    out[0] = (mm(t0[1], r0[...]) - mm(t0[0], x1)).astype(BF)

    @pl.when(z % 2 == 0)
    def _():
        out[1] = x1

    @pl.when(z == 1)
    def _():
        out[1] = x2

    @pl.when(z == 3)
    def _():
        out[1] = jnp.where(x_hi == 0, x3, x4)


PIECE = 2


def backward_kernel(parts, r, mats, own, got, *refs):
    bases, mts = refs[:parts], refs[parts : 2 * parts]
    leaf_out, root_out, sep_out, small, held, sems, small_sems = refs[2 * parts :]
    core = leaf_place()[0]
    left = jnp.where(core == 0, own[...], got[...])
    right = jnp.where(core == 0, got[...], own[...])
    parent = jnp.concatenate([left[0], right[0]], axis=1)
    small[0] = (mm(mats[1], r[...]) - mmt(mats[0], parent)).astype(BF)
    small[1] = jnp.where(core == 0, parent, jnp.concatenate([left[1], right[1]], axis=1))
    copies = [
        pltpu.make_async_copy(small.at[n], ref.at[0], small_sems.at[n])
        for n, ref in enumerate((root_out, sep_out))
    ]
    for copy in copies:
        copy.start()
    count = 24 // PIECE
    for step in range(count):
        part, at = divmod(step, count // parts)
        here = pl.ds(at * PIECE, PIECE)
        moved = mm(mts[part][here].reshape(PIECE * 256, 256), small[0])
        held[step] = (bases[part][here].astype(F32) + moved.reshape(PIECE, 256, 512)).astype(BF)
        copy = pltpu.make_async_copy(
            held.at[step], leaf_out.at[pl.ds(step * PIECE, PIECE)], sems.at[step]
        )
        copy.start()
        copies.append(copy)
    for copy in copies:
        copy.wait()


def backward(r, mats, own, got, bases, mts):
    return call(
        functools.partial(backward_kernel, len(bases)),
        [(24, 256, 512), (1, 256, 512), (1, 256, 512)],
        r,
        mats,
        own,
        got,
        *bases,
        *mts,
        scratch=[
            pltpu.VMEM((2, 256, 512), BF),
            pltpu.VMEM((24 // PIECE, PIECE, 256, 512), BF),
            pltpu.SemaphoreType.DMA((24 // PIECE,)),
            pltpu.SemaphoreType.DMA((2,)),
        ],
        out_specs=[ANY] * 3,
        flops=2**31,
        size=2**24,
        limit=14,
    )


def local(
    rhs_leaves,
    rhs_roots,
    rhs_seps,
    above_solution,
    leaf_inverse,
    leaf_update,
    leaf_rows,
    root_inverse,
    root_coupling,
    sep_inverse,
    sep_coupling,
):
    (w,) = call(
        pack_kernel,
        [(24, 48, 256)],
        leaf_inverse,
        leaf_update,
        scratch=[pltpu.SemaphoreType.DMA((2,))],
        limit=56,
        in_specs=[ANY] * 2,
    )
    (small,) = call(
        pack_small_kernel,
        [(8, 128, 256)],
        root_inverse,
        root_coupling,
        sep_inverse,
        sep_coupling,
        scratch=[pltpu.SemaphoreType.DMA((32,))],
        limit=56,
        in_specs=[ANY] * 4,
    )
    small = lax.all_to_all(small, "load", 0, 0)
    arrived = up(w), down(w), across(w), small
    staged = w, leaf_rows.reshape(24, 1, 128), rhs_seps
    staged = call(
        stage_kernel,
        [shape(v.shape, v.dtype) for v in staged],
        *staged,
        scratch=[pltpu.SemaphoreType.DMA((len(staged),))],
        in_specs=[ANY] * len(staged),
    )
    arrived, staged = lax.optimization_barrier((arrived, staged))
    a, b, c, small = arrived
    w, lists, rhs_seps = staged
    d, e, f = lax.optimization_barrier((up(a), across(a), down(c)))
    g, h = up(e[:HALF]), down(f[HALF:])
    blocks = (w, a, b, c, d, e, f)
    root_mats, keep, send = call(
        small_kernel, [(2, 256, 256), (3, 256, 256), (3, 256, 256)], small, rhs_seps, rhs_leaves
    )

    over_z = lambda v: [among(v, z_shift(k)) for k in (1, 2, 3)]
    even, odd, part = call(
        sides_kernel,
        [(3, 256, 256), (3, 256, 256), (2, 256, 256)],
        keep,
        among(send, CORES),
    )
    packs = over_z(part)
    m, inv, total = leaves_forward(
        (*blocks, g, h), rhs_leaves, lists
    )

    r_root, flow, send = call(
        root_kernel, [(256, 512), (256, 256), (256, 256)], rhs_roots, total, root_mats
    )
    packs2 = [among(v, CORES) for v in packs]
    theirs, even, odd = lax.optimization_barrier((among(send, CORES), even, odd))
    (top,) = call(
        choose_kernel, [(3, 256, 256)], odd, *packs, *packs2
    )
    far = among(top, X_HI)
    r0, flow, t0 = call(
        first_kernel,
        [(256, 256), (256, 256), (2, 256, 256)],
        even,
        flow,
        theirs,
    )
    flows = over_z(flow)
    held, flow = lax.optimization_barrier((inv, flow))
    parts = [prepare(8 * n, 8, held, m, rhs_leaves) for n in range(2)]
    flows, parts = lax.optimization_barrier((flows, parts))
    r, flow, t = call(
        middle_kernel,
        [(2, 256, 256), (256, 256), (2, 2, 256, 256)],
        odd,
        *packs,
        *packs2,
        flow,
        *flows,
    )
    theirs = among(flow, X_HI)
    held, flow = lax.optimization_barrier((held, flow))
    parts.append(prepare(16, 8, held, m, rhs_leaves))
    theirs, parts = lax.optimization_barrier((theirs, parts))
    (own,) = call(
        top_kernel,
        [(2, 256, 256)],
        flow,
        theirs,
        top,
        far,
        t0,
        t,
        r0,
        r,
        above_solution,
        scratch=[pltpu.VMEM((3, 256, 256), BF)] * 2,
    )
    return tuple(
        backward(
            r_root,
            root_mats,
            own,
            among(own, CORES),
            [p[0] for p in parts],
            [p[1] for p in parts],
        )
    )


def solution(mesh):
    rows = P("leaf", "load", None)
    columns = P("leaf", None, "load")
    in_specs = (columns, columns, columns, P(None, "load"), rows, rows, P("leaf", None)) + (rows,) * 4
    return jax.shard_map(
        local, mesh=mesh, in_specs=in_specs, out_specs=(columns,) * 3, check_vma=False
    )
```
